32 devices in a mesh: blk: 4 (over y, core), grp: 8 (over z, x).
Axes of the slice: x: 2, y: 2, z: 4, core: 2. Of those that a mesh axis runs over, the one named last changes fastest.
Arguments:
- picture_vectors_raw: bfloat16 [4096, 1152], P(('blk', 'grp')), may hold values from -0.1875 to 0.1875
- caption_vectors_raw: bfloat16 [4096, 1152], P(('blk', 'grp')), may hold values from -0.1875 to 0.1875
- logit_multiplier: float32 [1], replicated, may hold values from 60 to 120
- offset_term: float32 [1], replicated, may hold values from -3 to -1
- incoming_adjoint: float32 [1], replicated, may hold values from 100 to 300
Outputs:
- image_grad: float32 [4096, 1152], P(('blk', 'grp'))
- text_grad: float32 [4096, 1152], P(('blk', 'grp'))
The draws below stay inside these ranges and needn't reach their ends.
All inputs are finite; a program needn't handle non-finite values.
Results may differ from the reference program's by a relative error of at most 0.0079.
The reference program's roundings to bfloat16 on the way (of `image_half`, `text_half` and `coupling`) count: a program that leaves them out, or rounds other values in their place, can miss the bound.
Values may be sent and summed in bfloat16 or wider, within the bound.
A program may use at most 128 MiB of HBM per device.

```python
import math
import jax
import jax.numpy as jnp
from jax import lax

EMBED = 1152
MATCHED_SAMPLES = 4096


def levels(stream_key, dims, split, least, largest):
    loudness, own = 1.0, jax.random.fold_in(stream_key, 6)
    for dim, parts in split:
        heights = jnp.exp(jax.random.uniform(jax.random.fold_in(own, dim), (parts,), jnp.float32, least / len(split), largest / len(split)))
        loudness = loudness * jnp.repeat(heights, dims[dim] // parts).reshape([-1 if axis == dim else 1 for axis in range(len(dims))])
    return loudness


def gaussian(own_key, shape, deviation, bound, cuts=(), kind=jnp.bfloat16):
    entries = deviation * jax.random.normal(own_key, shape, jnp.float32)
    if cuts:
        entries = entries * levels(own_key, shape, cuts, -0.22, 0.18)
    return jnp.clip(entries, -bound, bound).astype(kind)


def setup_inputs(seed: int = 0) -> dict:
    streams_of = jax.random.split(jax.random.key(seed), 6)
    picture_vectors_raw = gaussian(streams_of[0], (MATCHED_SAMPLES, EMBED), EMBED ** -0.5, 0.1875, ((0, 32),))
    caption_vectors_raw = gaussian(streams_of[1], (MATCHED_SAMPLES, EMBED), EMBED ** -0.5, 0.1875, ((0, 32),))
    logit_multiplier = jnp.clip(jax.random.uniform(streams_of[2], (1,), jnp.float32, 60.0, 120.0), 60.0, 120.0)
    offset_term = jnp.clip(jax.random.uniform(streams_of[3], (1,), jnp.float32, -3.0, -1.0), -3.0, -1.0)
    incoming_adjoint = jnp.clip(jax.random.uniform(streams_of[4], (1,), jnp.float32, 100.0, 300.0), 100.0, 300.0)
    return dict(picture_vectors_raw=picture_vectors_raw, caption_vectors_raw=caption_vectors_raw, logit_multiplier=logit_multiplier, offset_term=offset_term, incoming_adjoint=incoming_adjoint)


def unit_rows(embedding):
    values = embedding.astype(jnp.float32)
    row_scale = lax.rsqrt(lax.optimization_barrier(jnp.mean(values * values, axis=1, keepdims=True)) + 1e-06) / math.sqrt(values.shape[1])
    return (values * row_scale, row_scale)

def unit_grad(unit_vals, row_scale, upstream_grad):
    return row_scale * (upstream_grad - unit_vals * lax.optimization_barrier(jnp.sum(unit_vals * upstream_grad, axis=1, keepdims=True)))

def reference(picture_vectors_raw, caption_vectors_raw, logit_multiplier, offset_term, incoming_adjoint):
    image_unit, image_scale = unit_rows(picture_vectors_raw)
    text_unit, text_scale = unit_rows(caption_vectors_raw)
    image_half = image_unit.astype(jnp.bfloat16)
    text_half = text_unit.astype(jnp.bfloat16)
    block_rows = math.gcd(MATCHED_SAMPLES, 1024)
    block_total = MATCHED_SAMPLES // block_rows
    derivative_multiplier = incoming_adjoint[0] * logit_multiplier[0] / MATCHED_SAMPLES
    target_position = jnp.arange(MATCHED_SAMPLES, dtype=jnp.int32)

    def advance(text_total, which):
        first_row = (which * block_rows).astype(jnp.int32)
        images = lax.dynamic_slice_in_dim(image_half, first_row, block_rows, 0)
        similarity_energies = lax.dot_general(images, text_half, (((1,), (1,)), ((), ())), preferred_element_type=jnp.float32)
        similarity_matrix = logit_multiplier[0] * similarity_energies + offset_term[0]
        source_position = first_row + jnp.arange(block_rows, dtype=jnp.int32)
        diag_mask = (source_position[:, None] == target_position[None, :]).astype(jnp.float32)
        coupling = (jax.nn.sigmoid(similarity_matrix) - diag_mask).astype(jnp.bfloat16)
        image_part = jnp.dot(coupling, text_half, preferred_element_type=jnp.float32)
        text_total = text_total + lax.dot_general(coupling, images, (((0,), (0,)), ((), ())), preferred_element_type=jnp.float32)
        return (text_total, image_part)
    start_total = jnp.zeros((MATCHED_SAMPLES, EMBED), jnp.float32)
    text_total, image_parts = lax.scan(advance, start_total, jnp.arange(block_total, dtype=jnp.int32))
    image_total = image_parts.reshape(MATCHED_SAMPLES, EMBED)
    image_grad = unit_grad(image_unit, image_scale, derivative_multiplier * image_total)
    text_grad = unit_grad(text_unit, text_scale, derivative_multiplier * text_total)
    return (image_grad, text_grad)
```

```python
import functools
import math

import jax
import jax.numpy as jnp
from jax import lax
from jax.experimental import pallas as pl
from jax.experimental.pallas import tpu as pltpu
from jax.sharding import PartitionSpec as P

MESH = pl.DeviceIdType.MESH
CHUNKS = 2
BF16 = jnp.bfloat16
F32 = jnp.float32


def unit_rows(embedding):
    values = embedding.astype(F32)
    row_scale = lax.rsqrt(jnp.mean(values * values, axis=1, keepdims=True) + 1e-06) / math.sqrt(
        values.shape[1]
    )
    return (values * row_scale, row_scale)


def unit_grad(unit_vals, row_scale, upstream_grad):
    return row_scale * (
        upstream_grad - unit_vals * jnp.sum(unit_vals * upstream_grad, axis=1, keepdims=True)
    )


def for_tiles(count, body):
    if count == 1:
        body(0)
    else:

        @pl.loop(0, count)
        def _(step):
            body(step)


def kernel(
    far,
    pairs,
    picture_ref,
    caption_ref,
    multiplier_ref,
    offset_ref,
    adjoint_ref,
    image_grad_ref,
    text_grad_ref,
    img,
    txt,
    coup,
    d_img,
    d_txt,
    send_x,
    recv_x,
    send_z,
    recv_z,
    send_c,
    recv_c,
    send_y,
    recv_y,
    send_w,
    recv_w,
    send_sem,
    recv_sem,
):
    rows = picture_ref.shape[0]
    part = rows // CHUNKS
    blk, grp = lax.axis_index("blk"), lax.axis_index("grp")
    y, core = lax.div(blk, 2), lax.rem(blk, 2)
    h, near, x = lax.div(grp, 4), lax.rem(lax.div(grp, 2), 2), lax.rem(grp, 2)
    at_x = (blk, h * 4 + near * 2 + (1 - x))
    at_near = (blk, h * 4 + (1 - near) * 2 + x)
    at_y = ((1 - y) * 2 + core, grp)
    at_core = (y * 2 + (1 - core), grp)
    at_far = [None] + [
        (blk, lax.rem(h + d, far) * 4 + near * 2 + x) for d in range(1, far)
    ]

    barrier = pltpu.get_barrier_semaphore()
    for peer in [at_x, at_near, at_y, at_core] + at_far[1:]:
        pl.semaphore_signal(barrier, inc=1, device_id=peer, device_id_type=MESH)

    image_unit, image_scale = unit_rows(picture_ref[...])
    text_unit, text_scale = unit_rows(caption_ref[...])
    img[pl.ds(0, rows), :] = image_unit.astype(BF16)
    txt[pl.ds(0, rows), :] = text_unit.astype(BF16)
    pl.semaphore_wait(barrier, 3 + far)

    started = []

    def send(src, src_slot, dst, dst_slot, chunk, peer):
        number = len(started)
        copy = pltpu.make_async_remote_copy(
            src_ref=src.at[pl.ds(src_slot * rows + chunk * part, part), :],
            dst_ref=dst.at[pl.ds(dst_slot * rows + chunk * part, part), :],
            send_sem=send_sem.at[number],
            recv_sem=recv_sem.at[number],
            device_id=peer,
            device_id_type=MESH,
        )
        copy.start()
        started.append(copy)
        return copy

    every = range(CHUNKS)
    img_z, txt_z, img_x, txt_y = {}, {}, {}, {}
    txt_c = []
    for c in every:
        for d in range(1, far):
            img_z[d, c] = send(img, 0, img, far - d, c, at_far[d])
        txt_z[c] = send(txt, 0, txt, 1, c, at_near)
        img_x[0, c] = send(img, 0, img, far, c, at_x)
        txt_y[0, c] = send(txt, 0, txt, 2, c, at_y)
    for c in every:
        txt_c.append(send(txt, 0, txt, 4, c, at_core))
    for c in every:
        for d in range(1, far):
            img_z[d, c].wait_recv()
            img_x[d, c] = send(img, far - d, img, 2 * far - d, c, at_x)
        txt_z[c].wait_recv()
        txt_y[1, c] = send(txt, 1, txt, 3, c, at_y)
        txt_c.append(send(txt, 1, txt, 5, c, at_core))
    for dz in (0, 1):
        for c in every:
            txt_y[dz, c].wait_recv()
            txt_c.append(send(txt, 2 + dz, txt, 6 + dz, c, at_core))
    for copy in img_x.values():
        copy.wait_recv()
    for copy in txt_c:
        copy.wait_recv()

    multiplier, offset = multiplier_ref[0], offset_ref[0]
    tile = 2 * rows

    def couple(step):
        lines = pl.ds(pl.multiple_of(step * tile, tile), tile)
        energies = lax.dot_general(
            img[lines, :], txt[...], (((1,), (1,)), ((), ())), preferred_element_type=F32
        )
        scores = multiplier * energies + offset
        coup[lines, :] = (1.0 / (1.0 + jnp.exp(-scores))).astype(BF16)

    for_tiles(far, couple)
    energies = lax.dot_general(
        img[pl.ds(0, rows), :],
        txt[pl.ds(0, rows), :],
        (((1,), (1,)), ((), ())),
        preferred_element_type=F32,
    )
    scores = multiplier * energies + offset
    same = lax.broadcasted_iota(jnp.int32, (rows, rows), 0) == lax.broadcasted_iota(
        jnp.int32, (rows, rows), 1
    )
    coup[pl.ds(0, rows), pl.ds(0, rows)] = (
        1.0 / (1.0 + jnp.exp(-scores)) - jnp.where(same, 1.0, 0.0)
    ).astype(BF16)

    def image_part(first, out):
        def body(step):
            start = pl.multiple_of(step * tile, tile)
            out[pl.ds(start, tile), :] = jnp.dot(
                coup[pl.ds(first + start, tile), :], txt[...], preferred_element_type=F32
            ).astype(out.dtype)

        for_tiles(far // 2, body)

    def text_part(slot, out, out_slot):
        out[pl.ds(out_slot * rows, tile), :] = lax.dot_general(
            coup[:, pl.ds(slot * rows, tile)],
            img[...],
            (((0,), (0,)), ((), ())),
            preferred_element_type=F32,
        ).astype(out.dtype)

    grad_c, grad_x, grad_y, grad_z, grad_w = {}, {}, {}, {}, {}
    text_part(6, send_c, 2)
    for dz in (1, 0):
        for c in every:
            grad_c[2 + dz, c] = send(send_c, 2 + dz, recv_c, 2 + dz, c, at_core)
    image_part(far * rows, send_x)
    for d in list(range(1, far)) + [0]:
        for c in every:
            grad_x[d, c] = send(send_x, d, recv_x, d, c, at_x)
    text_part(2, d_txt, 2)
    for dz in (1, 0):
        for c in every:
            grad_c[2 + dz, c].wait_recv()
            mine = pl.ds((2 + dz) * rows + c * part, part)
            send_y[pl.ds(dz * rows + c * part, part), :] = (
                d_txt[mine, :] + recv_c[mine, :].astype(F32)
            ).astype(BF16)
            grad_y[dz, c] = send(send_y, dz, recv_y, dz, c, at_y)
    text_part(4, send_c, 0)
    for dz in (1, 0):
        for c in every:
            grad_c[dz, c] = send(send_c, dz, recv_c, dz, c, at_core)
    image_part(0, d_img)
    text_part(0, d_txt, 0)

    for c in every:
        for d in range(1, far):
            grad_x[d, c].wait_recv()
            mine = pl.ds(d * rows + c * part, part)
            send_z[mine, :] = (d_img[mine, :] + recv_x[mine, :].astype(F32)).astype(BF16)
            grad_z[d, c] = send(send_z, d, recv_z, far - d, c, at_far[d])
        grad_c[1, c].wait_recv()
        grad_y[1, c].wait_recv()
        mine = pl.ds(rows + c * part, part)
        here = pl.ds(c * part, part)
        send_w[here, :] = (
            d_txt[mine, :] + recv_c[mine, :].astype(F32) + recv_y[mine, :].astype(F32)
        ).astype(BF16)
        grad_w[c] = send(send_w, 0, recv_w, 0, c, at_near)

    samples = rows * pairs
    derivative = adjoint_ref[0] * multiplier / samples
    for c in every:
        here = pl.ds(c * part, part)
        grad_x[0, c].wait_recv()
        total = d_img[here, :] + recv_x[here, :].astype(F32)
        for d in range(1, far):
            grad_z[d, c].wait_recv()
            total += recv_z[pl.ds((far - d) * rows + c * part, part), :].astype(F32)
        unit, scale = unit_rows(picture_ref[here, :])
        image_grad_ref[here, :] = unit_grad(unit, scale, derivative * total)
        grad_c[0, c].wait_recv()
        grad_y[0, c].wait_recv()
        grad_w[c].wait_recv()
        total = (
            d_txt[here, :]
            + recv_c[here, :].astype(F32)
            + recv_y[here, :].astype(F32)
            + recv_w[here, :].astype(F32)
        )
        unit, scale = unit_rows(caption_ref[here, :])
        text_grad_ref[here, :] = unit_grad(unit, scale, derivative * total)
    for copy in started:
        copy.wait_send()


def on_device(far, pairs, picture, caption, multiplier, offset, adjoint):
    rows, width = picture.shape
    copies = CHUNKS * (2 * (3 * far - 2 + 1) + 14 + 2 * far)
    vmem = pl.BlockSpec(memory_space=pltpu.VMEM)
    smem = pl.BlockSpec(memory_space=pltpu.SMEM)

    def slots(count, kind=BF16):
        return pltpu.VMEM((count * rows, width), kind)

    out = jax.ShapeDtypeStruct((rows, width), F32)
    return pl.pallas_call(
        functools.partial(kernel, far, pairs),
        out_shape=(out, out),
        in_specs=[vmem, vmem, smem, smem, smem],
        out_specs=(vmem, vmem),
        scratch_shapes=[
            slots(2 * far),
            slots(8),
            pltpu.VMEM((2 * far * rows, 8 * rows), BF16),
            slots(far, F32),
            slots(4, F32),
            slots(far),
            slots(far),
            slots(far),
            slots(far),
            slots(4),
            slots(4),
            slots(2),
            slots(2),
            slots(1),
            slots(1),
            pltpu.SemaphoreType.DMA((copies,)),
            pltpu.SemaphoreType.DMA((copies,)),
        ],
        compiler_params=pltpu.CompilerParams(
            collective_id=0, has_side_effects=True, vmem_limit_bytes=52 * 1024 * 1024
        ),
    )(picture, caption, multiplier, offset, adjoint)


def solution(mesh):
    placed = (P(("blk", "grp"), None), P(("blk", "grp"), None), P(), P(), P())
    pairs = mesh.shape["blk"] * mesh.shape["grp"]
    far = mesh.shape["grp"] // 4
    return jax.shard_map(
        functools.partial(on_device, far, pairs),
        mesh=mesh,
        in_specs=placed,
        out_specs=(P(("blk", "grp"), None), P(("blk", "grp"), None)),
        check_vma=False,
    )
```

```python
import functools
import math

import jax
import jax.numpy as jnp
from jax import lax
from jax.experimental import pallas as pl
from jax.experimental.pallas import tpu as pltpu
from jax.sharding import PartitionSpec as P

MESH = pl.DeviceIdType.MESH
CHUNKS = 4
BF16 = jnp.bfloat16
F32 = jnp.float32


def unit_rows(embedding):
    values = embedding.astype(F32)
    row_scale = lax.rsqrt(jnp.mean(values * values, axis=1, keepdims=True) + 1e-06) / math.sqrt(
        values.shape[1]
    )
    return (values * row_scale, row_scale)


def unit_grad(unit_vals, row_scale, upstream_grad):
    return row_scale * (
        upstream_grad - unit_vals * jnp.sum(unit_vals * upstream_grad, axis=1, keepdims=True)
    )


def for_tiles(first, end, body):
    if end - first == 1:
        body(first)
    else:

        @pl.loop(first, end)
        def _(step):
            body(step)


def kernel(
    far,
    pairs,
    picture_hbm,
    caption_hbm,
    multiplier_ref,
    offset_ref,
    adjoint_ref,
    image_grad_ref,
    text_grad_ref,
    picture_ref,
    caption_ref,
    img,
    txt,
    coup,
    d_img,
    d_txt,
    send_x,
    recv_x,
    send_z,
    recv_z,
    send_c,
    recv_c,
    send_y,
    recv_y,
    send_w,
    recv_w,
    load_sem,
    send_sem,
    recv_sem,
):
    rows = picture_ref.shape[0]
    part = rows // CHUNKS
    load_picture = pltpu.make_async_copy(picture_hbm, picture_ref, load_sem.at[0])
    load_caption = pltpu.make_async_copy(caption_hbm, caption_ref, load_sem.at[1])
    load_picture.start()
    load_caption.start()
    blk, grp = lax.axis_index("blk"), lax.axis_index("grp")
    y, core = lax.div(blk, 2), lax.rem(blk, 2)
    h, near, x = lax.div(grp, 4), lax.rem(lax.div(grp, 2), 2), lax.rem(grp, 2)
    at_x = (blk, h * 4 + near * 2 + (1 - x))
    at_near = (blk, h * 4 + (1 - near) * 2 + x)
    at_y = ((1 - y) * 2 + core, grp)
    at_core = (y * 2 + (1 - core), grp)
    at_far = [None] + [
        (blk, lax.rem(h + d, far) * 4 + near * 2 + x) for d in range(1, far)
    ]

    barrier = pltpu.get_barrier_semaphore()
    for peer in [at_x, at_near, at_y, at_core] + at_far[1:]:
        pl.semaphore_signal(barrier, inc=1, device_id=peer, device_id_type=MESH)

    load_picture.wait()
    img[pl.ds(0, rows), :] = unit_rows(picture_ref[...])[0].astype(BF16)
    load_caption.wait()
    txt[pl.ds(0, rows), :] = unit_rows(caption_ref[...])[0].astype(BF16)
    pl.semaphore_wait(barrier, 3 + far)

    started = []

    def send(src, src_slot, dst, dst_slot, chunk, peer):
        number = len(started)
        copy = pltpu.make_async_remote_copy(
            src_ref=src.at[pl.ds(src_slot * rows + chunk * part, part), :],
            dst_ref=dst.at[pl.ds(dst_slot * rows + chunk * part, part), :],
            send_sem=send_sem.at[number],
            recv_sem=recv_sem.at[number],
            device_id=peer,
            device_id_type=MESH,
        )
        copy.start()
        started.append(copy)
        return copy

    every = range(CHUNKS)
    img_z, txt_z, img_x, txt_y, txt_c = {}, {}, {}, {}, {}
    for c in every:
        for d in range(1, far):
            img_z[d, c] = send(img, 0, img, 2 * (far - d), c, at_far[d])
        txt_z[c] = send(txt, 0, txt, 4, c, at_near)
        img_x[0, c] = send(img, 0, img, 1, c, at_x)
        txt_y[0, c] = send(txt, 0, txt, 1, c, at_y)
    for c in every:
        txt_c[0, c] = send(txt, 0, txt, 2, c, at_core)

    multiplier, offset = multiplier_ref[0], offset_ref[0]
    tile = 2 * rows

    def sigmoid_tile(lines, columns):
        energies = lax.dot_general(
            img[lines, :], txt[columns, :], (((1,), (1,)), ((), ())), preferred_element_type=F32
        )
        return 1.0 / (1.0 + jnp.exp(-(multiplier * energies + offset)))

    def near_tiles():
        lines, columns = pl.ds(0, tile), pl.ds(0, 2 * tile)
        values = sigmoid_tile(lines, columns)
        same = lax.broadcasted_iota(jnp.int32, values.shape, 0) == lax.broadcasted_iota(
            jnp.int32, values.shape, 1
        )
        same = same & (lax.broadcasted_iota(jnp.int32, values.shape, 0) < rows)
        coup[lines, columns] = (values - jnp.where(same, 1.0, 0.0)).astype(BF16)

    for c in every:
        for d in range(1, far):
            img_z[d, c].wait_recv()
            img_x[d, c] = send(img, 2 * (far - d), img, 2 * (far - d) + 1, c, at_x)
        txt_z[c].wait_recv()
        txt_y[1, c] = send(txt, 4, txt, 5, c, at_y)
        txt_c[2, c] = send(txt, 4, txt, 6, c, at_core)
        if c == CHUNKS // 2:
            for e in every:
                txt_y[0, e].wait_recv()
                txt_c[1, e] = send(txt, 1, txt, 3, e, at_core)
    for c in every:
        img_x[0, c].wait_recv()
        txt_c[0, c].wait_recv()
        txt_c[1, c].wait_recv()
    near_tiles()
    for c in every:
        txt_y[1, c].wait_recv()
        txt_c[3, c] = send(txt, 5, txt, 7, c, at_core)
    for c in every:
        for d in range(1, far):
            img_x[d, c].wait_recv()
        txt_c[2, c].wait_recv()
        txt_c[3, c].wait_recv()

    def image_part(step):
        lines = pl.ds(pl.multiple_of(step * tile, tile), tile)
        total = jnp.dot(coup[lines, :], txt[...], preferred_element_type=F32)
        here = pl.ds(pl.multiple_of(step * rows, rows), rows)
        d_img[here, :] = total[:rows]
        send_x[here, :] = total[rows:].astype(BF16)

    def far_tiles(step):
        lines = pl.ds(pl.multiple_of(step * tile, tile), tile)
        coup[lines, :] = sigmoid_tile(lines, slice(None)).astype(BF16)
        image_part(step)

    def text_part(slot):
        return lax.dot_general(
            coup[:, pl.ds(slot * rows, tile)],
            img[...],
            (((0,), (0,)), ((), ())),
            preferred_element_type=F32,
        )

    grad_c, grad_x, grad_y, grad_z, grad_w = {}, {}, {}, {}, {}
    for_tiles(1, far, far_tiles)
    for c in every:
        for d in range(1, far):
            grad_x[d, c] = send(send_x, d, recv_x, d, c, at_x)
    lines, columns = pl.ds(0, tile), pl.ds(2 * tile, 2 * tile)
    coup[lines, columns] = sigmoid_tile(lines, columns).astype(BF16)
    for dz in (1, 0):
        send_c[pl.ds(2 * dz * rows, tile), :] = text_part(dz * 4 + 2).astype(BF16)
        for dy in (1, 0):
            for c in every:
                grad_c[dz, dy, c] = send(send_c, dz * 2 + dy, recv_c, dz * 2 + dy, c, at_core)
    image_part(0)
    for c in every:
        grad_x[0, c] = send(send_x, 0, recv_x, 0, c, at_x)
    for dz in (1, 0):
        d_txt[pl.ds(2 * dz * rows, tile), :] = text_part(dz * 4)
        for c in every:
            grad_c[dz, 1, c].wait_recv()
            mine = pl.ds((2 * dz + 1) * rows + c * part, part)
            send_y[pl.ds(dz * rows + c * part, part), :] = (
                d_txt[mine, :] + recv_c[mine, :].astype(F32)
            ).astype(BF16)
            grad_y[dz, c] = send(send_y, dz, recv_y, dz, c, at_y)

    for c in every:
        for d in range(1, far):
            grad_x[d, c].wait_recv()
            mine = pl.ds(d * rows + c * part, part)
            send_z[mine, :] = (d_img[mine, :] + recv_x[mine, :].astype(F32)).astype(BF16)
            grad_z[d, c] = send(send_z, d, recv_z, far - d, c, at_far[d])
        grad_c[1, 0, c].wait_recv()
        grad_y[1, c].wait_recv()
        mine = pl.ds(2 * rows + c * part, part)
        here = pl.ds(c * part, part)
        send_w[here, :] = (
            d_txt[mine, :]
            + recv_c[mine, :].astype(F32)
            + recv_y[pl.ds(rows + c * part, part), :].astype(F32)
        ).astype(BF16)
        grad_w[c] = send(send_w, 0, recv_w, 0, c, at_near)

    samples = rows * pairs
    derivative = adjoint_ref[0] * multiplier / samples
    for c in every:
        here = pl.ds(c * part, part)
        grad_x[0, c].wait_recv()
        total = d_img[here, :] + recv_x[here, :].astype(F32)
        for d in range(1, far):
            grad_z[d, c].wait_recv()
            total += recv_z[pl.ds((far - d) * rows + c * part, part), :].astype(F32)
        unit, scale = unit_rows(picture_ref[here, :])
        image_grad_ref[here, :] = unit_grad(unit, scale, derivative * total)
        grad_c[0, 0, c].wait_recv()
        grad_y[0, c].wait_recv()
        grad_w[c].wait_recv()
        total = (
            d_txt[here, :]
            + recv_c[here, :].astype(F32)
            + recv_y[here, :].astype(F32)
            + recv_w[here, :].astype(F32)
        )
        unit, scale = unit_rows(caption_ref[here, :])
        text_grad_ref[here, :] = unit_grad(unit, scale, derivative * total)
    for copy in started:
        copy.wait_send()


def on_device(far, pairs, picture, caption, multiplier, offset, adjoint):
    rows, width = picture.shape
    copies = CHUNKS * (4 * far + 12)
    vmem = pl.BlockSpec(memory_space=pltpu.VMEM)
    hbm = pl.BlockSpec(memory_space=pltpu.HBM)
    smem = pl.BlockSpec(memory_space=pltpu.SMEM)

    def slots(count, kind=BF16):
        return pltpu.VMEM((count * rows, width), kind)

    out = jax.ShapeDtypeStruct((rows, width), F32)
    return pl.pallas_call(
        functools.partial(kernel, far, pairs),
        out_shape=(out, out),
        in_specs=[hbm, hbm, smem, smem, smem],
        out_specs=(vmem, vmem),
        scratch_shapes=[
            slots(1),
            slots(1),
            slots(2 * far),
            slots(8),
            pltpu.VMEM((2 * far * rows, 8 * rows), BF16),
            slots(far, F32),
            slots(4, F32),
            slots(far),
            slots(far),
            slots(far),
            slots(far),
            slots(4),
            slots(4),
            slots(2),
            slots(2),
            slots(1),
            slots(1),
            pltpu.SemaphoreType.DMA((2,)),
            pltpu.SemaphoreType.DMA((copies,)),
            pltpu.SemaphoreType.DMA((copies,)),
        ],
        compiler_params=pltpu.CompilerParams(
            collective_id=0, has_side_effects=True, vmem_limit_bytes=63 * 1024 * 1024
        ),
    )(picture, caption, multiplier, offset, adjoint)


def solution(mesh):
    placed = (P(("blk", "grp"), None), P(("blk", "grp"), None), P(), P(), P())
    pairs = mesh.shape["blk"] * mesh.shape["grp"]
    far = mesh.shape["grp"] // 4
    return jax.shard_map(
        functools.partial(on_device, far, pairs),
        mesh=mesh,
        in_specs=placed,
        out_specs=(P(("blk", "grp"), None), P(("blk", "grp"), None)),
        check_vma=False,
    )
```

```python
import functools
import math

import jax
import jax.numpy as jnp
from jax import lax
from jax.experimental import pallas as pl
from jax.experimental.pallas import tpu as pltpu
from jax.sharding import PartitionSpec as P

MESH = pl.DeviceIdType.MESH
CHUNKS = 4
AHEAD = 2
BF16 = jnp.bfloat16
F32 = jnp.float32


def unit_rows(embedding):
    values = embedding.astype(F32)
    row_scale = lax.rsqrt(jnp.mean(values * values, axis=1, keepdims=True) + 1e-06) / math.sqrt(
        values.shape[1]
    )
    return (values * row_scale, row_scale)


def unit_grad(unit_vals, row_scale, upstream_grad):
    return row_scale * (
        upstream_grad - unit_vals * jnp.sum(unit_vals * upstream_grad, axis=1, keepdims=True)
    )


def for_tiles(first, end, body):
    if end - first == 1:
        body(first)
    else:

        @pl.loop(first, end)
        def _(step):
            body(step)


def kernel(
    far,
    pairs,
    picture_hbm,
    caption_hbm,
    multiplier_ref,
    offset_ref,
    adjoint_ref,
    image_grad_ref,
    text_grad_ref,
    picture_ref,
    caption_ref,
    img,
    txt,
    coup,
    d_img,
    d_txt,
    send_x,
    recv_x,
    send_z,
    recv_z,
    send_c,
    recv_c,
    send_y,
    recv_y,
    send_w,
    recv_w,
    load_sem,
    send_sem,
    recv_sem,
):
    rows = picture_ref.shape[0]
    part = rows // CHUNKS
    load_picture = pltpu.make_async_copy(picture_hbm, picture_ref, load_sem.at[0])
    load_caption = pltpu.make_async_copy(caption_hbm, caption_ref, load_sem.at[1])
    load_picture.start()
    load_caption.start()
    blk, grp = lax.axis_index("blk"), lax.axis_index("grp")
    y, core = lax.div(blk, 2), lax.rem(blk, 2)
    h, near, x = lax.div(grp, 4), lax.rem(lax.div(grp, 2), 2), lax.rem(grp, 2)
    at_x = (blk, h * 4 + near * 2 + (1 - x))
    at_near = (blk, h * 4 + (1 - near) * 2 + x)
    at_y = ((1 - y) * 2 + core, grp)
    at_core = (y * 2 + (1 - core), grp)
    at_far = [None] + [
        (blk, lax.rem(h + d, far) * 4 + near * 2 + x) for d in range(1, far)
    ]

    barrier = pltpu.get_barrier_semaphore()
    for peer in [at_x, at_near, at_y, at_core] + at_far[1:]:
        pl.semaphore_signal(barrier, inc=1, device_id=peer, device_id_type=MESH)

    load_picture.wait()
    img[pl.ds(0, rows), :] = unit_rows(picture_ref[...])[0].astype(BF16)
    load_caption.wait()
    txt[pl.ds(0, rows), :] = unit_rows(caption_ref[...])[0].astype(BF16)
    pl.semaphore_wait(barrier, 3 + far)

    started = {}

    def send(src, src_slot, dst, dst_slot, chunk, peer):
        number = len(started)
        copy = pltpu.make_async_remote_copy(
            src_ref=src.at[pl.ds(src_slot * rows + chunk * part, part), :],
            dst_ref=dst.at[pl.ds(dst_slot * rows + chunk * part, part), :],
            send_sem=send_sem.at[number],
            recv_sem=recv_sem.at[number],
            device_id=peer,
            device_id_type=MESH,
        )
        copy.start()
        started[number] = copy
        return copy

    def sent(copy):
        copy.wait_send()
        for number in started:
            if started[number] is copy:
                started[number] = None

    every = range(CHUNKS)
    img_z, txt_z, img_x, txt_y, txt_c = {}, {}, {}, {}, {}

    def start_z(c):
        for d in range(1, far):
            if c > 0:
                sent(img_z[d, c - 1])
            img_z[d, c] = send(img, 0, img, 2 * (far - d), c, at_far[d])
        if c > 0:
            sent(txt_z[c - 1])
        txt_z[c] = send(txt, 0, txt, 4, c, at_near)

    start_z(0)
    for c in every:
        img_x[0, c] = send(img, 0, img, 1, c, at_x)
        txt_y[0, c] = send(txt, 0, txt, 1, c, at_y)
    for c in every:
        txt_c[0, c] = send(txt, 0, txt, 2, c, at_core)

    multiplier, offset = multiplier_ref[0], offset_ref[0]
    tile = 2 * rows

    def sigmoid_tile(lines, columns):
        energies = lax.dot_general(
            img[lines, :], txt[columns, :], (((1,), (1,)), ((), ())), preferred_element_type=F32
        )
        return 1.0 / (1.0 + jnp.exp(-(multiplier * energies + offset)))

    def near_tiles():
        lines, columns = pl.ds(0, tile), pl.ds(0, 2 * tile)
        values = sigmoid_tile(lines, columns)
        same = lax.broadcasted_iota(jnp.int32, values.shape, 0) == lax.broadcasted_iota(
            jnp.int32, values.shape, 1
        )
        same = same & (lax.broadcasted_iota(jnp.int32, values.shape, 0) < rows)
        coup[lines, columns] = (values - jnp.where(same, 1.0, 0.0)).astype(BF16)

    for c in every:
        if c + 1 < CHUNKS:
            start_z(c + 1)
        for d in range(1, far):
            img_z[d, c].wait_recv()
            img_x[d, c] = send(img, 2 * (far - d), img, 2 * (far - d) + 1, c, at_x)
        txt_z[c].wait_recv()
        txt_y[1, c] = send(txt, 4, txt, 5, c, at_y)
        txt_c[2, c] = send(txt, 4, txt, 6, c, at_core)
        if c == CHUNKS // 2:
            for e in every:
                txt_y[0, e].wait_recv()
                txt_c[1, e] = send(txt, 1, txt, 3, e, at_core)
    for c in every:
        img_x[0, c].wait_recv()
        txt_c[0, c].wait_recv()
        txt_c[1, c].wait_recv()
    near_tiles()
    for c in every:
        txt_y[1, c].wait_recv()
        txt_c[3, c] = send(txt, 5, txt, 7, c, at_core)
    for c in every:
        for d in range(1, far):
            img_x[d, c].wait_recv()
        txt_c[2, c].wait_recv()
        txt_c[3, c].wait_recv()

    def image_part(step):
        lines = pl.ds(pl.multiple_of(step * tile, tile), tile)
        total = jnp.dot(coup[lines, :], txt[...], preferred_element_type=F32)
        here = pl.ds(pl.multiple_of(step * rows, rows), rows)
        d_img[here, :] = total[:rows]
        send_x[here, :] = total[rows:].astype(BF16)

    def far_tiles(step):
        lines = pl.ds(pl.multiple_of(step * tile, tile), tile)
        coup[lines, :] = sigmoid_tile(lines, slice(None)).astype(BF16)
        image_part(step)

    def text_part(slot):
        return lax.dot_general(
            coup[:, pl.ds(slot * rows, tile)],
            img[...],
            (((0,), (0,)), ((), ())),
            preferred_element_type=F32,
        )

    grad_c, grad_x, grad_y, grad_z, grad_w = {}, {}, {}, {}, {}
    order_x = [[(d, c) for d in range(1, far)] for c in every] + [[(0, c)] for c in every]
    order_y = [(1, c) for c in every] + [(0, c) for c in every]

    def start_x(k):
        if k >= AHEAD:
            for key in order_x[k - AHEAD]:
                sent(grad_x[key])
        for d, c in order_x[k]:
            grad_x[d, c] = send(send_x, d, recv_x, d, c, at_x)

    def start_y(k):
        if k >= AHEAD:
            sent(grad_y[order_y[k - AHEAD]])
        dz, c = order_y[k]
        grad_y[dz, c] = send(send_y, dz, recv_y, dz, c, at_y)

    def core_part(dz):
        send_c[pl.ds(2 * dz * rows, tile), :] = text_part(dz * 4 + 2).astype(BF16)
        for dy in (1, 0):
            for c in every:
                grad_c[dz, dy, c] = send(send_c, dz * 2 + dy, recv_c, dz * 2 + dy, c, at_core)

    def own_part(dz):
        d_txt[pl.ds(2 * dz * rows, tile), :] = text_part(dz * 4)

    def y_sum(dz, c):
        grad_c[dz, 1, c].wait_recv()
        mine = pl.ds((2 * dz + 1) * rows + c * part, part)
        send_y[pl.ds(dz * rows + c * part, part), :] = (
            d_txt[mine, :] + recv_c[mine, :].astype(F32)
        ).astype(BF16)

    for_tiles(1, far, far_tiles)
    for k in range(AHEAD):
        start_x(k)
    lines, columns = pl.ds(0, tile), pl.ds(2 * tile, 2 * tile)
    coup[lines, columns] = sigmoid_tile(lines, columns).astype(BF16)
    core_part(1)
    own_part(1)
    core_part(0)
    for c in every:
        y_sum(1, c)
        if c < AHEAD:
            start_y(c)
    image_part(0)
    own_part(0)
    for c in every:
        y_sum(0, c)

    for c in every:
        start_x(c + AHEAD)
        for d in range(1, far):
            grad_x[d, c].wait_recv()
            mine = pl.ds(d * rows + c * part, part)
            send_z[mine, :] = (d_img[mine, :] + recv_x[mine, :].astype(F32)).astype(BF16)
            grad_z[d, c] = send(send_z, d, recv_z, far - d, c, at_far[d])
        start_y(c + AHEAD)
        grad_c[1, 0, c].wait_recv()
        grad_y[1, c].wait_recv()
        mine = pl.ds(2 * rows + c * part, part)
        here = pl.ds(c * part, part)
        send_w[here, :] = (
            d_txt[mine, :]
            + recv_c[mine, :].astype(F32)
            + recv_y[pl.ds(rows + c * part, part), :].astype(F32)
        ).astype(BF16)
        grad_w[c] = send(send_w, 0, recv_w, 0, c, at_near)
    for k in range(CHUNKS + AHEAD, 2 * CHUNKS):
        start_x(k)
        start_y(k)

    samples = rows * pairs
    derivative = adjoint_ref[0] * multiplier / samples
    for c in every:
        here = pl.ds(c * part, part)
        grad_x[0, c].wait_recv()
        total = d_img[here, :] + recv_x[here, :].astype(F32)
        for d in range(1, far):
            grad_z[d, c].wait_recv()
            total += recv_z[pl.ds((far - d) * rows + c * part, part), :].astype(F32)
        unit, scale = unit_rows(picture_ref[here, :])
        image_grad_ref[here, :] = unit_grad(unit, scale, derivative * total)
        grad_c[0, 0, c].wait_recv()
        grad_y[0, c].wait_recv()
        grad_w[c].wait_recv()
        total = (
            d_txt[here, :]
            + recv_c[here, :].astype(F32)
            + recv_y[here, :].astype(F32)
            + recv_w[here, :].astype(F32)
        )
        unit, scale = unit_rows(caption_ref[here, :])
        text_grad_ref[here, :] = unit_grad(unit, scale, derivative * total)
    for copy in started.values():
        if copy is not None:
            copy.wait_send()


def on_device(far, pairs, picture, caption, multiplier, offset, adjoint):
    rows, width = picture.shape
    copies = CHUNKS * (4 * far + 12)
    vmem = pl.BlockSpec(memory_space=pltpu.VMEM)
    hbm = pl.BlockSpec(memory_space=pltpu.HBM)
    smem = pl.BlockSpec(memory_space=pltpu.SMEM)

    def slots(count, kind=BF16):
        return pltpu.VMEM((count * rows, width), kind)

    out = jax.ShapeDtypeStruct((rows, width), F32)
    return pl.pallas_call(
        functools.partial(kernel, far, pairs),
        out_shape=(out, out),
        in_specs=[hbm, hbm, smem, smem, smem],
        out_specs=(vmem, vmem),
        scratch_shapes=[
            slots(1),
            slots(1),
            slots(2 * far),
            slots(8),
            pltpu.VMEM((2 * far * rows, 8 * rows), BF16),
            slots(far, F32),
            slots(4, F32),
            slots(far),
            slots(far),
            slots(far),
            slots(far),
            slots(4),
            slots(4),
            slots(2),
            slots(2),
            slots(1),
            slots(1),
            pltpu.SemaphoreType.DMA((2,)),
            pltpu.SemaphoreType.DMA((copies,)),
            pltpu.SemaphoreType.DMA((copies,)),
        ],
        compiler_params=pltpu.CompilerParams(
            collective_id=0, has_side_effects=True, vmem_limit_bytes=52 * 1024 * 1024
        ),
    )(picture, caption, multiplier, offset, adjoint)


def solution(mesh):
    placed = (P(("blk", "grp"), None), P(("blk", "grp"), None), P(), P(), P())
    pairs = mesh.shape["blk"] * mesh.shape["grp"]
    far = mesh.shape["grp"] // 4
    return jax.shard_map(
        functools.partial(on_device, far, pairs),
        mesh=mesh,
        in_specs=placed,
        out_specs=(P(("blk", "grp"), None), P(("blk", "grp"), None)),
        check_vma=False,
    )
```

```python
import functools
import math

import jax
import jax.numpy as jnp
from jax import lax
from jax.experimental import pallas as pl
from jax.experimental.pallas import tpu as pltpu
from jax.sharding import PartitionSpec as P

MESH = pl.DeviceIdType.MESH
CHUNKS = 4
AHEAD = 4
BF16 = jnp.bfloat16
F32 = jnp.float32


def unit_rows(embedding):
    values = embedding.astype(F32)
    row_scale = lax.rsqrt(jnp.mean(values * values, axis=1, keepdims=True) + 1e-06) / math.sqrt(
        values.shape[1]
    )
    return (values * row_scale, row_scale)


def unit_grad(unit_vals, row_scale, upstream_grad):
    return row_scale * (
        upstream_grad - unit_vals * jnp.sum(unit_vals * upstream_grad, axis=1, keepdims=True)
    )


def for_tiles(first, end, body):
    if end - first == 1:
        body(first)
    else:

        @pl.loop(first, end)
        def _(step):
            body(step)


def kernel(
    far,
    pairs,
    picture_hbm,
    caption_hbm,
    multiplier_ref,
    offset_ref,
    adjoint_ref,
    image_grad_ref,
    text_grad_ref,
    picture_ref,
    caption_ref,
    img,
    txt,
    coup,
    d_img,
    d_txt,
    send_x,
    recv_x,
    send_z,
    recv_z,
    send_c,
    recv_c,
    send_y,
    recv_y,
    send_w,
    recv_w,
    load_sem,
    send_sem,
    recv_sem,
):
    rows = picture_ref.shape[0]
    part = rows // CHUNKS
    load_picture = pltpu.make_async_copy(picture_hbm, picture_ref, load_sem.at[0])
    load_caption = pltpu.make_async_copy(caption_hbm, caption_ref, load_sem.at[1])
    load_picture.start()
    load_caption.start()
    blk, grp = lax.axis_index("blk"), lax.axis_index("grp")
    y, core = lax.div(blk, 2), lax.rem(blk, 2)
    h, near, x = lax.div(grp, 4), lax.rem(lax.div(grp, 2), 2), lax.rem(grp, 2)
    at_x = (blk, h * 4 + near * 2 + (1 - x))
    at_near = (blk, h * 4 + (1 - near) * 2 + x)
    at_y = ((1 - y) * 2 + core, grp)
    at_core = (y * 2 + (1 - core), grp)
    at_far = [None] + [
        (blk, lax.rem(h + d, far) * 4 + near * 2 + x) for d in range(1, far)
    ]

    barrier = pltpu.get_barrier_semaphore()
    for peer in [at_x, at_near, at_y, at_core] + at_far[1:]:
        pl.semaphore_signal(barrier, inc=1, device_id=peer, device_id_type=MESH)

    load_picture.wait()
    img[pl.ds(0, rows), :] = unit_rows(picture_ref[...])[0].astype(BF16)
    load_caption.wait()
    txt[pl.ds(0, rows), :] = unit_rows(caption_ref[...])[0].astype(BF16)
    pl.semaphore_wait(barrier, 3 + far)

    started = {}

    def send(src, src_slot, dst, dst_slot, chunk, peer):
        number = len(started)
        copy = pltpu.make_async_remote_copy(
            src_ref=src.at[pl.ds(src_slot * rows + chunk * part, part), :],
            dst_ref=dst.at[pl.ds(dst_slot * rows + chunk * part, part), :],
            send_sem=send_sem.at[number],
            recv_sem=recv_sem.at[number],
            device_id=peer,
            device_id_type=MESH,
        )
        copy.start()
        started[number] = copy
        return copy

    def sent(copy):
        copy.wait_send()
        for number in started:
            if started[number] is copy:
                started[number] = None

    every = range(CHUNKS)
    img_z, txt_z, img_x, txt_y, txt_c = {}, {}, {}, {}, {}

    def start_z(c):
        for d in range(1, far):
            if c > 0:
                sent(img_z[d, c - 1])
            img_z[d, c] = send(img, 0, img, 2 * (far - d), c, at_far[d])
        if c > 0:
            sent(txt_z[c - 1])
        txt_z[c] = send(txt, 0, txt, 4, c, at_near)

    start_z(0)
    for c in every:
        img_x[0, c] = send(img, 0, img, 1, c, at_x)
        txt_y[0, c] = send(txt, 0, txt, 1, c, at_y)
    for c in every:
        txt_c[0, c] = send(txt, 0, txt, 2, c, at_core)

    multiplier, offset = multiplier_ref[0], offset_ref[0]
    tile = 2 * rows

    def sigmoid_tile(lines, columns):
        energies = lax.dot_general(
            img[lines, :], txt[columns, :], (((1,), (1,)), ((), ())), preferred_element_type=F32
        )
        return 1.0 / (1.0 + jnp.exp(-(multiplier * energies + offset)))

    def near_tiles():
        lines, columns = pl.ds(0, tile), pl.ds(0, 2 * tile)
        values = sigmoid_tile(lines, columns)
        same = lax.broadcasted_iota(jnp.int32, values.shape, 0) == lax.broadcasted_iota(
            jnp.int32, values.shape, 1
        )
        same = same & (lax.broadcasted_iota(jnp.int32, values.shape, 0) < rows)
        coup[lines, columns] = (values - jnp.where(same, 1.0, 0.0)).astype(BF16)

    for c in every:
        if c + 1 < CHUNKS:
            start_z(c + 1)
        for d in range(1, far):
            img_z[d, c].wait_recv()
            img_x[d, c] = send(img, 2 * (far - d), img, 2 * (far - d) + 1, c, at_x)
        txt_z[c].wait_recv()
        txt_y[1, c] = send(txt, 4, txt, 5, c, at_y)
        txt_c[2, c] = send(txt, 4, txt, 6, c, at_core)
        if c == CHUNKS // 2:
            for e in every:
                txt_y[0, e].wait_recv()
                txt_c[1, e] = send(txt, 1, txt, 3, e, at_core)
    for c in every:
        img_x[0, c].wait_recv()
        txt_c[0, c].wait_recv()
        txt_c[1, c].wait_recv()
    near_tiles()
    for c in every:
        txt_y[1, c].wait_recv()
        txt_c[3, c] = send(txt, 5, txt, 7, c, at_core)
    for c in every:
        for d in range(1, far):
            img_x[d, c].wait_recv()
        txt_c[2, c].wait_recv()
        txt_c[3, c].wait_recv()

    def image_part(step):
        lines = pl.ds(pl.multiple_of(step * tile, tile), tile)
        total = jnp.dot(coup[lines, :], txt[...], preferred_element_type=F32)
        here = pl.ds(pl.multiple_of(step * rows, rows), rows)
        d_img[here, :] = total[:rows]
        send_x[here, :] = total[rows:].astype(BF16)

    def far_tiles(step):
        lines = pl.ds(pl.multiple_of(step * tile, tile), tile)
        coup[lines, :] = sigmoid_tile(lines, slice(None)).astype(BF16)
        image_part(step)

    def text_part(slot):
        return lax.dot_general(
            coup[:, pl.ds(slot * rows, tile)],
            img[...],
            (((0,), (0,)), ((), ())),
            preferred_element_type=F32,
        )

    grad_c, grad_x, grad_y, grad_z, grad_w = {}, {}, {}, {}, {}
    order_x = [[(d, c) for d in range(1, far)] for c in every] + [[(0, c)] for c in every]
    order_y = [(1, c) for c in every] + [(0, c) for c in every]

    def start_x(k):
        if k >= AHEAD:
            for key in order_x[k - AHEAD]:
                sent(grad_x[key])
        for d, c in order_x[k]:
            grad_x[d, c] = send(send_x, d, recv_x, d, c, at_x)

    def start_y(k):
        if k >= AHEAD:
            sent(grad_y[order_y[k - AHEAD]])
        dz, c = order_y[k]
        grad_y[dz, c] = send(send_y, dz, recv_y, dz, c, at_y)

    def core_part(dz):
        send_c[pl.ds(2 * dz * rows, tile), :] = text_part(dz * 4 + 2).astype(BF16)
        for dy in (1, 0):
            for c in every:
                grad_c[dz, dy, c] = send(send_c, dz * 2 + dy, recv_c, dz * 2 + dy, c, at_core)

    def own_part(dz):
        d_txt[pl.ds(2 * dz * rows, tile), :] = text_part(dz * 4)

    def y_sum(dz, c):
        grad_c[dz, 1, c].wait_recv()
        mine = pl.ds((2 * dz + 1) * rows + c * part, part)
        send_y[pl.ds(dz * rows + c * part, part), :] = (
            d_txt[mine, :] + recv_c[mine, :].astype(F32)
        ).astype(BF16)

    def forward_z(c):
        for d in range(1, far):
            grad_x[d, c].wait_recv()
            mine = pl.ds(d * rows + c * part, part)
            send_z[mine, :] = (d_img[mine, :] + recv_x[mine, :].astype(F32)).astype(BF16)
            grad_z[d, c] = send(send_z, d, recv_z, far - d, c, at_far[d])

    def forward_near(c):
        grad_c[1, 0, c].wait_recv()
        grad_y[1, c].wait_recv()
        mine = pl.ds(2 * rows + c * part, part)
        here = pl.ds(c * part, part)
        send_w[here, :] = (
            d_txt[mine, :]
            + recv_c[mine, :].astype(F32)
            + recv_y[pl.ds(rows + c * part, part), :].astype(F32)
        ).astype(BF16)
        grad_w[c] = send(send_w, 0, recv_w, 0, c, at_near)

    for_tiles(1, far, far_tiles)
    for c in every:
        start_x(c)
    lines, columns = pl.ds(0, tile), pl.ds(2 * tile, 2 * tile)
    coup[lines, columns] = sigmoid_tile(lines, columns).astype(BF16)
    core_part(1)
    own_part(1)
    for c in every:
        y_sum(1, c)
        start_y(c)
    image_part(0)
    for c in range(CHUNKS // 2):
        forward_z(c)
        start_x(CHUNKS + c)
    core_part(0)
    for c in range(CHUNKS // 2, CHUNKS):
        forward_z(c)
        start_x(CHUNKS + c)
    own_part(0)
    for c in every:
        y_sum(0, c)
        start_y(CHUNKS + c)
        forward_near(c)

    samples = rows * pairs
    derivative = adjoint_ref[0] * multiplier / samples
    for c in every:
        here = pl.ds(c * part, part)
        grad_x[0, c].wait_recv()
        total = d_img[here, :] + recv_x[here, :].astype(F32)
        for d in range(1, far):
            grad_z[d, c].wait_recv()
            total += recv_z[pl.ds((far - d) * rows + c * part, part), :].astype(F32)
        unit, scale = unit_rows(picture_ref[here, :])
        image_grad_ref[here, :] = unit_grad(unit, scale, derivative * total)
        grad_c[0, 0, c].wait_recv()
        grad_y[0, c].wait_recv()
        grad_w[c].wait_recv()
        total = (
            d_txt[here, :]
            + recv_c[here, :].astype(F32)
            + recv_y[here, :].astype(F32)
            + recv_w[here, :].astype(F32)
        )
        unit, scale = unit_rows(caption_ref[here, :])
        text_grad_ref[here, :] = unit_grad(unit, scale, derivative * total)
    for copy in started.values():
        if copy is not None:
            copy.wait_send()


def on_device(far, pairs, picture, caption, multiplier, offset, adjoint):
    rows, width = picture.shape
    copies = CHUNKS * (4 * far + 12)
    vmem = pl.BlockSpec(memory_space=pltpu.VMEM)
    hbm = pl.BlockSpec(memory_space=pltpu.HBM)
    smem = pl.BlockSpec(memory_space=pltpu.SMEM)

    def slots(count, kind=BF16):
        return pltpu.VMEM((count * rows, width), kind)

    out = jax.ShapeDtypeStruct((rows, width), F32)
    grads = pl.pallas_call(
        functools.partial(kernel, far, pairs),
        out_shape=(out, out),
        in_specs=[hbm, hbm, smem, smem, smem],
        out_specs=(vmem, vmem),
        scratch_shapes=[
            slots(1),
            slots(1),
            slots(2 * far),
            slots(8),
            pltpu.VMEM((2 * far * rows, 8 * rows), BF16),
            slots(far, F32),
            slots(4, F32),
            slots(far),
            slots(far),
            slots(far),
            slots(far),
            slots(4),
            slots(4),
            slots(2),
            slots(2),
            slots(1),
            slots(1),
            pltpu.SemaphoreType.DMA((2,)),
            pltpu.SemaphoreType.DMA((copies,)),
            pltpu.SemaphoreType.DMA((copies,)),
        ],
        compiler_params=pltpu.CompilerParams(
            collective_id=0, has_side_effects=True, vmem_limit_bytes=52 * 1024 * 1024
        ),
    )(
        pltpu.with_memory_space_constraint(picture, pltpu.HBM),
        pltpu.with_memory_space_constraint(caption, pltpu.HBM),
        multiplier,
        offset,
        adjoint,
    )
    return copied_out(*grads)


def copy_out_kernel(image_ref, text_ref, image_out, text_out, sem):
    copies = [
        pltpu.make_async_copy(image_ref, image_out, sem.at[0]),
        pltpu.make_async_copy(text_ref, text_out, sem.at[1]),
    ]
    for copy in copies:
        copy.start()
    for copy in copies:
        copy.wait()


def copied_out(image_grad, text_grad):
    hbm = pl.BlockSpec(memory_space=pltpu.HBM)
    anywhere = pl.BlockSpec(memory_space=pl.ANY)
    return pl.pallas_call(
        copy_out_kernel,
        out_shape=(
            jax.ShapeDtypeStruct(image_grad.shape, F32),
            jax.ShapeDtypeStruct(text_grad.shape, F32),
        ),
        in_specs=[anywhere, anywhere],
        out_specs=(hbm, hbm),
        scratch_shapes=[pltpu.SemaphoreType.DMA((2,))],
        compiler_params=pltpu.CompilerParams(vmem_limit_bytes=4 * 1024 * 1024),
    )(image_grad, text_grad)


def solution(mesh):
    placed = (P(("blk", "grp"), None), P(("blk", "grp"), None), P(), P(), P())
    pairs = mesh.shape["blk"] * mesh.shape["grp"]
    far = mesh.shape["grp"] // 4
    return jax.shard_map(
        functools.partial(on_device, far, pairs),
        mesh=mesh,
        in_specs=placed,
        out_specs=(P(("blk", "grp"), None), P(("blk", "grp"), None)),
        check_vma=False,
    )
```

```python
import functools
import math

import jax
import jax.numpy as jnp
from jax import lax
from jax.experimental import pallas as pl
from jax.experimental.pallas import tpu as pltpu
from jax.sharding import PartitionSpec as P

MESH = pl.DeviceIdType.MESH
CHUNKS = 8
AHEAD = 8
Z_AHEAD = 2
BF16 = jnp.bfloat16
F32 = jnp.float32


def unit_rows(embedding):
    values = embedding.astype(F32)
    row_scale = lax.rsqrt(jnp.mean(values * values, axis=1, keepdims=True) + 1e-06) / math.sqrt(
        values.shape[1]
    )
    return (values * row_scale, row_scale)


def unit_grad(unit_vals, row_scale, upstream_grad):
    return row_scale * (
        upstream_grad - unit_vals * jnp.sum(unit_vals * upstream_grad, axis=1, keepdims=True)
    )


def for_tiles(first, end, body):
    if end - first == 1:
        body(first)
    else:

        @pl.loop(first, end)
        def _(step):
            body(step)


def kernel(
    far,
    pairs,
    picture_hbm,
    caption_hbm,
    multiplier_ref,
    offset_ref,
    adjoint_ref,
    image_grad_ref,
    text_grad_ref,
    picture_ref,
    caption_ref,
    img,
    txt,
    coup,
    d_img,
    d_txt,
    send_x,
    recv_x,
    send_z,
    recv_z,
    send_c,
    recv_c,
    send_y,
    recv_y,
    send_w,
    recv_w,
    load_sem,
    send_sem,
    recv_sem,
):
    rows = picture_ref.shape[0]
    part = rows // CHUNKS
    load_picture = pltpu.make_async_copy(picture_hbm, picture_ref, load_sem.at[0])
    load_caption = pltpu.make_async_copy(caption_hbm, caption_ref, load_sem.at[1])
    load_picture.start()
    load_caption.start()
    blk, grp = lax.axis_index("blk"), lax.axis_index("grp")
    y, core = lax.div(blk, 2), lax.rem(blk, 2)
    h, near, x = lax.div(grp, 4), lax.rem(lax.div(grp, 2), 2), lax.rem(grp, 2)
    at_x = (blk, h * 4 + near * 2 + (1 - x))
    at_near = (blk, h * 4 + (1 - near) * 2 + x)
    at_y = ((1 - y) * 2 + core, grp)
    at_core = (y * 2 + (1 - core), grp)
    at_far = [None] + [
        (blk, lax.rem(h + d, far) * 4 + near * 2 + x) for d in range(1, far)
    ]

    barrier = pltpu.get_barrier_semaphore()
    for peer in [at_x, at_near, at_y, at_core] + at_far[1:]:
        pl.semaphore_signal(barrier, inc=1, device_id=peer, device_id_type=MESH)

    load_picture.wait()
    img[pl.ds(0, rows), :] = unit_rows(picture_ref[...])[0].astype(BF16)
    load_caption.wait()
    txt[pl.ds(0, rows), :] = unit_rows(caption_ref[...])[0].astype(BF16)
    pl.semaphore_wait(barrier, 3 + far)

    started = {}

    def send(src, src_slot, dst, dst_slot, chunk, peer):
        number = len(started)
        copy = pltpu.make_async_remote_copy(
            src_ref=src.at[pl.ds(src_slot * rows + chunk * part, part), :],
            dst_ref=dst.at[pl.ds(dst_slot * rows + chunk * part, part), :],
            send_sem=send_sem.at[number],
            recv_sem=recv_sem.at[number],
            device_id=peer,
            device_id_type=MESH,
        )
        copy.start()
        started[number] = copy
        return copy

    def sent(copy):
        copy.wait_send()
        for number in started:
            if started[number] is copy:
                started[number] = None

    every = range(CHUNKS)
    img_z, txt_z, img_x, txt_y, txt_c = {}, {}, {}, {}, {}

    def start_z(c):
        for d in range(1, far):
            if c >= Z_AHEAD:
                sent(img_z[d, c - Z_AHEAD])
            img_z[d, c] = send(img, 0, img, 2 * (far - d), c, at_far[d])
        if c >= Z_AHEAD:
            sent(txt_z[c - Z_AHEAD])
        txt_z[c] = send(txt, 0, txt, 4, c, at_near)

    for c in range(Z_AHEAD):
        start_z(c)
    for c in every:
        img_x[0, c] = send(img, 0, img, 1, c, at_x)
        txt_y[0, c] = send(txt, 0, txt, 1, c, at_y)
    for c in every:
        txt_c[0, c] = send(txt, 0, txt, 2, c, at_core)

    multiplier, offset = multiplier_ref[0], offset_ref[0]
    tile = 2 * rows

    def sigmoid_tile(lines, columns):
        energies = lax.dot_general(
            img[lines, :], txt[columns, :], (((1,), (1,)), ((), ())), preferred_element_type=F32
        )
        return 1.0 / (1.0 + jnp.exp(-(multiplier * energies + offset)))

    def near_tiles():
        lines, columns = pl.ds(0, tile), pl.ds(0, 2 * tile)
        values = sigmoid_tile(lines, columns)
        same = lax.broadcasted_iota(jnp.int32, values.shape, 0) == lax.broadcasted_iota(
            jnp.int32, values.shape, 1
        )
        same = same & (lax.broadcasted_iota(jnp.int32, values.shape, 0) < rows)
        coup[lines, columns] = (values - jnp.where(same, 1.0, 0.0)).astype(BF16)

    for c in every:
        if c + Z_AHEAD < CHUNKS:
            start_z(c + Z_AHEAD)
        for d in range(1, far):
            img_z[d, c].wait_recv()
            img_x[d, c] = send(img, 2 * (far - d), img, 2 * (far - d) + 1, c, at_x)
        txt_z[c].wait_recv()
        txt_y[1, c] = send(txt, 4, txt, 5, c, at_y)
        txt_c[2, c] = send(txt, 4, txt, 6, c, at_core)
        if c == CHUNKS // 2:
            for e in every:
                txt_y[0, e].wait_recv()
                txt_c[1, e] = send(txt, 1, txt, 3, e, at_core)
    for c in every:
        img_x[0, c].wait_recv()
        txt_c[0, c].wait_recv()
        txt_c[1, c].wait_recv()
    near_tiles()
    for c in every:
        txt_y[1, c].wait_recv()
        txt_c[3, c] = send(txt, 5, txt, 7, c, at_core)
    for c in every:
        for d in range(1, far):
            img_x[d, c].wait_recv()
        txt_c[2, c].wait_recv()
        txt_c[3, c].wait_recv()

    def image_part(step):
        lines = pl.ds(pl.multiple_of(step * tile, tile), tile)
        total = jnp.dot(coup[lines, :], txt[...], preferred_element_type=F32)
        here = pl.ds(pl.multiple_of(step * rows, rows), rows)
        d_img[here, :] = total[:rows]
        send_x[here, :] = total[rows:].astype(BF16)

    def far_tiles(step):
        lines = pl.ds(pl.multiple_of(step * tile, tile), tile)
        coup[lines, :] = sigmoid_tile(lines, slice(None)).astype(BF16)
        image_part(step)

    def text_part(slot):
        return lax.dot_general(
            coup[:, pl.ds(slot * rows, tile)],
            img[...],
            (((0,), (0,)), ((), ())),
            preferred_element_type=F32,
        )

    grad_c, grad_x, grad_y, grad_z, grad_w = {}, {}, {}, {}, {}
    order_x = [[(d, c) for d in range(1, far)] for c in every] + [[(0, c)] for c in every]
    order_y = [(1, c) for c in every] + [(0, c) for c in every]

    def start_x(k):
        if k >= AHEAD:
            for key in order_x[k - AHEAD]:
                sent(grad_x[key])
        for d, c in order_x[k]:
            grad_x[d, c] = send(send_x, d, recv_x, d, c, at_x)

    def start_y(k):
        if k >= AHEAD:
            sent(grad_y[order_y[k - AHEAD]])
        dz, c = order_y[k]
        grad_y[dz, c] = send(send_y, dz, recv_y, dz, c, at_y)

    def core_part(dz):
        send_c[pl.ds(2 * dz * rows, tile), :] = text_part(dz * 4 + 2).astype(BF16)
        for dy in (1, 0):
            for c in every:
                grad_c[dz, dy, c] = send(send_c, dz * 2 + dy, recv_c, dz * 2 + dy, c, at_core)

    def own_part(dz):
        d_txt[pl.ds(2 * dz * rows, tile), :] = text_part(dz * 4)

    def y_sum(dz, c):
        grad_c[dz, 1, c].wait_recv()
        mine = pl.ds((2 * dz + 1) * rows + c * part, part)
        send_y[pl.ds(dz * rows + c * part, part), :] = (
            d_txt[mine, :] + recv_c[mine, :].astype(F32)
        ).astype(BF16)

    def forward_z(c):
        for d in range(1, far):
            grad_x[d, c].wait_recv()
            mine = pl.ds(d * rows + c * part, part)
            send_z[mine, :] = (d_img[mine, :] + recv_x[mine, :].astype(F32)).astype(BF16)
            grad_z[d, c] = send(send_z, d, recv_z, far - d, c, at_far[d])

    def forward_near(c):
        grad_c[1, 0, c].wait_recv()
        grad_y[1, c].wait_recv()
        mine = pl.ds(2 * rows + c * part, part)
        here = pl.ds(c * part, part)
        send_w[here, :] = (
            d_txt[mine, :]
            + recv_c[mine, :].astype(F32)
            + recv_y[pl.ds(rows + c * part, part), :].astype(F32)
        ).astype(BF16)
        grad_w[c] = send(send_w, 0, recv_w, 0, c, at_near)

    for_tiles(1, far, far_tiles)
    for c in every:
        start_x(c)
    lines, columns = pl.ds(0, tile), pl.ds(2 * tile, 2 * tile)
    coup[lines, columns] = sigmoid_tile(lines, columns).astype(BF16)
    core_part(1)
    own_part(1)
    for c in every:
        y_sum(1, c)
        start_y(c)
    image_part(0)
    for c in range(CHUNKS // 2):
        forward_z(c)
        start_x(CHUNKS + c)
    core_part(0)
    for c in range(CHUNKS // 2, CHUNKS):
        forward_z(c)
        start_x(CHUNKS + c)
    own_part(0)
    for c in every:
        y_sum(0, c)
        start_y(CHUNKS + c)
        forward_near(c)

    samples = rows * pairs
    derivative = adjoint_ref[0] * multiplier / samples
    for c in every:
        here = pl.ds(c * part, part)
        grad_x[0, c].wait_recv()
        total = d_img[here, :] + recv_x[here, :].astype(F32)
        for d in range(1, far):
            grad_z[d, c].wait_recv()
            total += recv_z[pl.ds((far - d) * rows + c * part, part), :].astype(F32)
        unit, scale = unit_rows(picture_ref[here, :])
        image_grad_ref[here, :] = unit_grad(unit, scale, derivative * total)
        grad_c[0, 0, c].wait_recv()
        grad_y[0, c].wait_recv()
        grad_w[c].wait_recv()
        total = (
            d_txt[here, :]
            + recv_c[here, :].astype(F32)
            + recv_y[here, :].astype(F32)
            + recv_w[here, :].astype(F32)
        )
        unit, scale = unit_rows(caption_ref[here, :])
        text_grad_ref[here, :] = unit_grad(unit, scale, derivative * total)
    for copy in started.values():
        if copy is not None:
            copy.wait_send()


def on_device(far, pairs, picture, caption, multiplier, offset, adjoint):
    rows, width = picture.shape
    copies = CHUNKS * (4 * far + 12)
    vmem = pl.BlockSpec(memory_space=pltpu.VMEM)
    hbm = pl.BlockSpec(memory_space=pltpu.HBM)
    smem = pl.BlockSpec(memory_space=pltpu.SMEM)

    def slots(count, kind=BF16):
        return pltpu.VMEM((count * rows, width), kind)

    out = jax.ShapeDtypeStruct((rows, width), F32)
    grads = pl.pallas_call(
        functools.partial(kernel, far, pairs),
        out_shape=(out, out),
        in_specs=[hbm, hbm, smem, smem, smem],
        out_specs=(vmem, vmem),
        scratch_shapes=[
            slots(1),
            slots(1),
            slots(2 * far),
            slots(8),
            pltpu.VMEM((2 * far * rows, 8 * rows), BF16),
            slots(far, F32),
            slots(4, F32),
            slots(far),
            slots(far),
            slots(far),
            slots(far),
            slots(4),
            slots(4),
            slots(2),
            slots(2),
            slots(1),
            slots(1),
            pltpu.SemaphoreType.DMA((2,)),
            pltpu.SemaphoreType.DMA((copies,)),
            pltpu.SemaphoreType.DMA((copies,)),
        ],
        compiler_params=pltpu.CompilerParams(
            collective_id=0, has_side_effects=True, vmem_limit_bytes=52 * 1024 * 1024
        ),
    )(
        pltpu.with_memory_space_constraint(picture, pltpu.HBM),
        pltpu.with_memory_space_constraint(caption, pltpu.HBM),
        multiplier,
        offset,
        adjoint,
    )
    return copied_out(*grads)


def copy_out_kernel(image_ref, text_ref, image_out, text_out, sem):
    copies = [
        pltpu.make_async_copy(image_ref, image_out, sem.at[0]),
        pltpu.make_async_copy(text_ref, text_out, sem.at[1]),
    ]
    for copy in copies:
        copy.start()
    for copy in copies:
        copy.wait()


def copied_out(image_grad, text_grad):
    hbm = pl.BlockSpec(memory_space=pltpu.HBM)
    anywhere = pl.BlockSpec(memory_space=pl.ANY)
    return pl.pallas_call(
        copy_out_kernel,
        out_shape=(
            jax.ShapeDtypeStruct(image_grad.shape, F32),
            jax.ShapeDtypeStruct(text_grad.shape, F32),
        ),
        in_specs=[anywhere, anywhere],
        out_specs=(hbm, hbm),
        scratch_shapes=[pltpu.SemaphoreType.DMA((2,))],
        compiler_params=pltpu.CompilerParams(vmem_limit_bytes=4 * 1024 * 1024),
    )(image_grad, text_grad)


def solution(mesh):
    placed = (P(("blk", "grp"), None), P(("blk", "grp"), None), P(), P(), P())
    pairs = mesh.shape["blk"] * mesh.shape["grp"]
    far = mesh.shape["grp"] // 4
    return jax.shard_map(
        functools.partial(on_device, far, pairs),
        mesh=mesh,
        in_specs=placed,
        out_specs=(P(("blk", "grp"), None), P(("blk", "grp"), None)),
        check_vma=False,
    )
```

```python
import functools
import math

import jax
import jax.numpy as jnp
from jax import lax
from jax.experimental import pallas as pl
from jax.experimental.pallas import tpu as pltpu
from jax.sharding import PartitionSpec as P

MESH = pl.DeviceIdType.MESH
CHUNKS = 2
AHEAD = 2
Z_AHEAD = 2
BF16 = jnp.bfloat16
F32 = jnp.float32


def unit_rows(embedding):
    values = embedding.astype(F32)
    row_scale = lax.rsqrt(jnp.mean(values * values, axis=1, keepdims=True) + 1e-06) / math.sqrt(
        values.shape[1]
    )
    return (values * row_scale, row_scale)


def unit_grad(unit_vals, row_scale, upstream_grad):
    return row_scale * (
        upstream_grad - unit_vals * jnp.sum(unit_vals * upstream_grad, axis=1, keepdims=True)
    )


def for_tiles(first, end, body):
    if end - first == 1:
        body(first)
    else:

        @pl.loop(first, end)
        def _(step):
            body(step)


def kernel(
    far,
    pairs,
    picture_hbm,
    caption_hbm,
    multiplier_ref,
    offset_ref,
    adjoint_ref,
    image_grad_ref,
    text_grad_ref,
    picture_ref,
    caption_ref,
    img,
    txt,
    coup,
    d_img,
    d_txt,
    send_x,
    recv_x,
    send_z,
    recv_z,
    send_c,
    recv_c,
    send_y,
    recv_y,
    send_w,
    recv_w,
    load_sem,
    send_sem,
    recv_sem,
):
    rows = picture_ref.shape[0]
    part = rows // CHUNKS
    load_picture = pltpu.make_async_copy(picture_hbm, picture_ref, load_sem.at[0])
    load_caption = pltpu.make_async_copy(caption_hbm, caption_ref, load_sem.at[1])
    load_picture.start()
    load_caption.start()
    blk, grp = lax.axis_index("blk"), lax.axis_index("grp")
    y, core = lax.div(blk, 2), lax.rem(blk, 2)
    h, near, x = lax.div(grp, 4), lax.rem(lax.div(grp, 2), 2), lax.rem(grp, 2)
    at_x = (blk, h * 4 + near * 2 + (1 - x))
    at_near = (blk, h * 4 + (1 - near) * 2 + x)
    at_y = ((1 - y) * 2 + core, grp)
    at_core = (y * 2 + (1 - core), grp)
    at_far = [None] + [
        (blk, lax.rem(h + d, far) * 4 + near * 2 + x) for d in range(1, far)
    ]

    barrier = pltpu.get_barrier_semaphore()
    for peer in [at_x, at_near, at_y, at_core] + at_far[1:]:
        pl.semaphore_signal(barrier, inc=1, device_id=peer, device_id_type=MESH)

    load_picture.wait()
    img[pl.ds(0, rows), :] = unit_rows(picture_ref[...])[0].astype(BF16)
    load_caption.wait()
    txt[pl.ds(0, rows), :] = unit_rows(caption_ref[...])[0].astype(BF16)
    pl.semaphore_wait(barrier, 3 + far)

    started = {}

    def send(src, src_slot, dst, dst_slot, chunk, peer):
        number = len(started)
        copy = pltpu.make_async_remote_copy(
            src_ref=src.at[pl.ds(src_slot * rows + chunk * part, part), :],
            dst_ref=dst.at[pl.ds(dst_slot * rows + chunk * part, part), :],
            send_sem=send_sem.at[number],
            recv_sem=recv_sem.at[number],
            device_id=peer,
            device_id_type=MESH,
        )
        copy.start()
        started[number] = copy
        return copy

    def sent(copy):
        copy.wait_send()
        for number in started:
            if started[number] is copy:
                started[number] = None

    every = range(CHUNKS)
    img_z, txt_z, img_x, txt_y, txt_c = {}, {}, {}, {}, {}

    def start_z(c):
        for d in range(1, far):
            if c >= Z_AHEAD:
                sent(img_z[d, c - Z_AHEAD])
            img_z[d, c] = send(img, 0, img, 2 * (far - d), c, at_far[d])
        if c >= Z_AHEAD:
            sent(txt_z[c - Z_AHEAD])
        txt_z[c] = send(txt, 0, txt, 4, c, at_near)

    for c in range(Z_AHEAD):
        start_z(c)
    for c in every:
        img_x[0, c] = send(img, 0, img, 1, c, at_x)
        txt_y[0, c] = send(txt, 0, txt, 1, c, at_y)
    for c in every:
        txt_c[0, c] = send(txt, 0, txt, 2, c, at_core)

    multiplier, offset = multiplier_ref[0], offset_ref[0]
    tile = 2 * rows

    def sigmoid_tile(lines, columns):
        energies = lax.dot_general(
            img[lines, :], txt[columns, :], (((1,), (1,)), ((), ())), preferred_element_type=F32
        )
        return 1.0 / (1.0 + jnp.exp(-(multiplier * energies + offset)))

    def near_tiles():
        lines, columns = pl.ds(0, tile), pl.ds(0, 2 * tile)
        values = sigmoid_tile(lines, columns)
        same = lax.broadcasted_iota(jnp.int32, values.shape, 0) == lax.broadcasted_iota(
            jnp.int32, values.shape, 1
        )
        same = same & (lax.broadcasted_iota(jnp.int32, values.shape, 0) < rows)
        coup[lines, columns] = (values - jnp.where(same, 1.0, 0.0)).astype(BF16)

    for c in every:
        if c + Z_AHEAD < CHUNKS:
            start_z(c + Z_AHEAD)
        for d in range(1, far):
            img_z[d, c].wait_recv()
            img_x[d, c] = send(img, 2 * (far - d), img, 2 * (far - d) + 1, c, at_x)
        txt_z[c].wait_recv()
        txt_y[1, c] = send(txt, 4, txt, 5, c, at_y)
        txt_c[2, c] = send(txt, 4, txt, 6, c, at_core)
        if c == CHUNKS // 2:
            for e in every:
                txt_y[0, e].wait_recv()
                txt_c[1, e] = send(txt, 1, txt, 3, e, at_core)
    for c in every:
        img_x[0, c].wait_recv()
        txt_c[0, c].wait_recv()
        txt_c[1, c].wait_recv()
    near_tiles()
    for c in every:
        txt_y[1, c].wait_recv()
        txt_c[3, c] = send(txt, 5, txt, 7, c, at_core)
    for c in every:
        for d in range(1, far):
            img_x[d, c].wait_recv()
        txt_c[2, c].wait_recv()
        txt_c[3, c].wait_recv()

    def image_part(step):
        lines = pl.ds(pl.multiple_of(step * tile, tile), tile)
        total = jnp.dot(coup[lines, :], txt[...], preferred_element_type=F32)
        here = pl.ds(pl.multiple_of(step * rows, rows), rows)
        d_img[here, :] = total[:rows]
        send_x[here, :] = total[rows:].astype(BF16)

    def far_tiles(step):
        lines = pl.ds(pl.multiple_of(step * tile, tile), tile)
        coup[lines, :] = sigmoid_tile(lines, slice(None)).astype(BF16)
        image_part(step)

    def text_part(slot):
        return lax.dot_general(
            coup[:, pl.ds(slot * rows, tile)],
            img[...],
            (((0,), (0,)), ((), ())),
            preferred_element_type=F32,
        )

    grad_c, grad_x, grad_y, grad_z, grad_w = {}, {}, {}, {}, {}
    order_x = [[(d, c) for d in range(1, far)] for c in every] + [[(0, c)] for c in every]
    order_y = [(1, c) for c in every] + [(0, c) for c in every]

    def start_x(k):
        if k >= AHEAD:
            for key in order_x[k - AHEAD]:
                sent(grad_x[key])
        for d, c in order_x[k]:
            grad_x[d, c] = send(send_x, d, recv_x, d, c, at_x)

    def start_y(k):
        if k >= AHEAD:
            sent(grad_y[order_y[k - AHEAD]])
        dz, c = order_y[k]
        grad_y[dz, c] = send(send_y, dz, recv_y, dz, c, at_y)

    def core_part(dz):
        send_c[pl.ds(2 * dz * rows, tile), :] = text_part(dz * 4 + 2).astype(BF16)
        for dy in (1, 0):
            for c in every:
                grad_c[dz, dy, c] = send(send_c, dz * 2 + dy, recv_c, dz * 2 + dy, c, at_core)

    def own_part(dz):
        d_txt[pl.ds(2 * dz * rows, tile), :] = text_part(dz * 4)

    def y_sum(dz, c):
        grad_c[dz, 1, c].wait_recv()
        mine = pl.ds((2 * dz + 1) * rows + c * part, part)
        send_y[pl.ds(dz * rows + c * part, part), :] = (
            d_txt[mine, :] + recv_c[mine, :].astype(F32)
        ).astype(BF16)

    def forward_z(c):
        for d in range(1, far):
            grad_x[d, c].wait_recv()
            mine = pl.ds(d * rows + c * part, part)
            send_z[mine, :] = (d_img[mine, :] + recv_x[mine, :].astype(F32)).astype(BF16)
            grad_z[d, c] = send(send_z, d, recv_z, far - d, c, at_far[d])

    def forward_near(c):
        grad_c[1, 0, c].wait_recv()
        grad_y[1, c].wait_recv()
        mine = pl.ds(2 * rows + c * part, part)
        here = pl.ds(c * part, part)
        send_w[here, :] = (
            d_txt[mine, :]
            + recv_c[mine, :].astype(F32)
            + recv_y[pl.ds(rows + c * part, part), :].astype(F32)
        ).astype(BF16)
        grad_w[c] = send(send_w, 0, recv_w, 0, c, at_near)

    for_tiles(1, far, far_tiles)
    for c in every:
        start_x(c)
    lines, columns = pl.ds(0, tile), pl.ds(2 * tile, 2 * tile)
    coup[lines, columns] = sigmoid_tile(lines, columns).astype(BF16)
    core_part(1)
    own_part(1)
    for c in every:
        y_sum(1, c)
        start_y(c)
    image_part(0)
    for c in range(CHUNKS // 2):
        forward_z(c)
        start_x(CHUNKS + c)
    core_part(0)
    for c in range(CHUNKS // 2, CHUNKS):
        forward_z(c)
        start_x(CHUNKS + c)
    own_part(0)
    for c in every:
        y_sum(0, c)
        start_y(CHUNKS + c)
        forward_near(c)

    samples = rows * pairs
    derivative = adjoint_ref[0] * multiplier / samples
    for c in every:
        here = pl.ds(c * part, part)
        grad_x[0, c].wait_recv()
        total = d_img[here, :] + recv_x[here, :].astype(F32)
        for d in range(1, far):
            grad_z[d, c].wait_recv()
            total += recv_z[pl.ds((far - d) * rows + c * part, part), :].astype(F32)
        unit, scale = unit_rows(picture_ref[here, :])
        image_grad_ref[here, :] = unit_grad(unit, scale, derivative * total)
        grad_c[0, 0, c].wait_recv()
        grad_y[0, c].wait_recv()
        grad_w[c].wait_recv()
        total = (
            d_txt[here, :]
            + recv_c[here, :].astype(F32)
            + recv_y[here, :].astype(F32)
            + recv_w[here, :].astype(F32)
        )
        unit, scale = unit_rows(caption_ref[here, :])
        text_grad_ref[here, :] = unit_grad(unit, scale, derivative * total)
    for copy in started.values():
        if copy is not None:
            copy.wait_send()


def on_device(far, pairs, picture, caption, multiplier, offset, adjoint):
    rows, width = picture.shape
    copies = CHUNKS * (4 * far + 12)
    vmem = pl.BlockSpec(memory_space=pltpu.VMEM)
    hbm = pl.BlockSpec(memory_space=pltpu.HBM)
    smem = pl.BlockSpec(memory_space=pltpu.SMEM)

    def slots(count, kind=BF16):
        return pltpu.VMEM((count * rows, width), kind)

    out = jax.ShapeDtypeStruct((rows, width), F32)
    grads = pl.pallas_call(
        functools.partial(kernel, far, pairs),
        out_shape=(out, out),
        in_specs=[hbm, hbm, smem, smem, smem],
        out_specs=(vmem, vmem),
        scratch_shapes=[
            slots(1),
            slots(1),
            slots(2 * far),
            slots(8),
            pltpu.VMEM((2 * far * rows, 8 * rows), BF16),
            slots(far, F32),
            slots(4, F32),
            slots(far),
            slots(far),
            slots(far),
            slots(far),
            slots(4),
            slots(4),
            slots(2),
            slots(2),
            slots(1),
            slots(1),
            pltpu.SemaphoreType.DMA((2,)),
            pltpu.SemaphoreType.DMA((copies,)),
            pltpu.SemaphoreType.DMA((copies,)),
        ],
        compiler_params=pltpu.CompilerParams(
            collective_id=0, has_side_effects=True, vmem_limit_bytes=52 * 1024 * 1024
        ),
    )(
        pltpu.with_memory_space_constraint(picture, pltpu.HBM),
        pltpu.with_memory_space_constraint(caption, pltpu.HBM),
        multiplier,
        offset,
        adjoint,
    )
    return copied_out(*grads)


def copy_out_kernel(image_ref, text_ref, image_out, text_out, sem):
    copies = [
        pltpu.make_async_copy(image_ref, image_out, sem.at[0]),
        pltpu.make_async_copy(text_ref, text_out, sem.at[1]),
    ]
    for copy in copies:
        copy.start()
    for copy in copies:
        copy.wait()


def copied_out(image_grad, text_grad):
    hbm = pl.BlockSpec(memory_space=pltpu.HBM)
    anywhere = pl.BlockSpec(memory_space=pl.ANY)
    return pl.pallas_call(
        copy_out_kernel,
        out_shape=(
            jax.ShapeDtypeStruct(image_grad.shape, F32),
            jax.ShapeDtypeStruct(text_grad.shape, F32),
        ),
        in_specs=[anywhere, anywhere],
        out_specs=(hbm, hbm),
        scratch_shapes=[pltpu.SemaphoreType.DMA((2,))],
        compiler_params=pltpu.CompilerParams(vmem_limit_bytes=4 * 1024 * 1024),
    )(image_grad, text_grad)


def solution(mesh):
    placed = (P(("blk", "grp"), None), P(("blk", "grp"), None), P(), P(), P())
    pairs = mesh.shape["blk"] * mesh.shape["grp"]
    far = mesh.shape["grp"] // 4
    return jax.shard_map(
        functools.partial(on_device, far, pairs),
        mesh=mesh,
        in_specs=placed,
        out_specs=(P(("blk", "grp"), None), P(("blk", "grp"), None)),
        check_vma=False,
    )
```

```python
import functools
import math

import jax
import jax.numpy as jnp
from jax import lax
from jax.experimental import pallas as pl
from jax.experimental.pallas import tpu as pltpu
from jax.sharding import PartitionSpec as P

MESH = pl.DeviceIdType.MESH
CHUNKS = 2
AHEAD = 2
Z_AHEAD = 1
BF16 = jnp.bfloat16
F32 = jnp.float32


def unit_rows(embedding):
    values = embedding.astype(F32)
    row_scale = lax.rsqrt(jnp.mean(values * values, axis=1, keepdims=True) + 1e-06) / math.sqrt(
        values.shape[1]
    )
    return (values * row_scale, row_scale)


def unit_grad(unit_vals, row_scale, upstream_grad):
    return row_scale * (
        upstream_grad - unit_vals * jnp.sum(unit_vals * upstream_grad, axis=1, keepdims=True)
    )


def for_tiles(first, end, body):
    if end - first == 1:
        body(first)
    else:

        @pl.loop(first, end)
        def _(step):
            body(step)


def kernel(
    far,
    pairs,
    picture_hbm,
    caption_hbm,
    multiplier_ref,
    offset_ref,
    adjoint_ref,
    image_grad_ref,
    text_grad_ref,
    picture_ref,
    caption_ref,
    img,
    txt,
    coup,
    d_img,
    d_txt,
    send_x,
    recv_x,
    send_z,
    recv_z,
    send_c,
    recv_c,
    send_y,
    recv_y,
    send_w,
    recv_w,
    load_sem,
    send_sem,
    recv_sem,
):
    rows = picture_ref.shape[0]
    part = rows // CHUNKS
    load_picture = pltpu.make_async_copy(picture_hbm, picture_ref, load_sem.at[0])
    load_caption = pltpu.make_async_copy(caption_hbm, caption_ref, load_sem.at[1])
    load_picture.start()
    load_caption.start()
    blk, grp = lax.axis_index("blk"), lax.axis_index("grp")
    y, core = lax.div(blk, 2), lax.rem(blk, 2)
    h, near, x = lax.div(grp, 4), lax.rem(lax.div(grp, 2), 2), lax.rem(grp, 2)
    at_x = (blk, h * 4 + near * 2 + (1 - x))
    at_near = (blk, h * 4 + (1 - near) * 2 + x)
    at_y = ((1 - y) * 2 + core, grp)
    at_core = (y * 2 + (1 - core), grp)
    at_far = [None] + [
        (blk, lax.rem(h + d, far) * 4 + near * 2 + x) for d in range(1, far)
    ]

    barrier = pltpu.get_barrier_semaphore()
    for peer in [at_x, at_near, at_y, at_core] + at_far[1:]:
        pl.semaphore_signal(barrier, inc=1, device_id=peer, device_id_type=MESH)

    started = {}

    def send(src, src_slot, dst, dst_slot, chunk, peer):
        number = len(started)
        first, length = (0, rows) if chunk is None else (chunk * part, part)
        copy = pltpu.make_async_remote_copy(
            src_ref=src.at[pl.ds(src_slot * rows + first, length), :],
            dst_ref=dst.at[pl.ds(dst_slot * rows + first, length), :],
            send_sem=send_sem.at[number],
            recv_sem=recv_sem.at[number],
            device_id=peer,
            device_id_type=MESH,
        )
        copy.start()
        started[number] = copy
        return copy

    def sent(copy):
        copy.wait_send()
        for number in started:
            if started[number] is copy:
                started[number] = None

    every = range(CHUNKS)
    img_z, txt_z, img_x, txt_y, txt_c = {}, {}, {}, {}, {}

    def start_img_z(c):
        for d in range(1, far):
            if c >= Z_AHEAD:
                sent(img_z[d, c - Z_AHEAD])
            img_z[d, c] = send(img, 0, img, 2 * (far - d), c, at_far[d])

    def start_txt_z(c):
        if c >= Z_AHEAD:
            sent(txt_z[c - Z_AHEAD])
        txt_z[c] = send(txt, 0, txt, 4, c, at_near)

    load_picture.wait()
    img[pl.ds(0, rows), :] = unit_rows(picture_ref[...])[0].astype(BF16)
    pl.semaphore_wait(barrier, 3 + far)
    for c in range(Z_AHEAD):
        start_img_z(c)
    for c in every:
        img_x[0, c] = send(img, 0, img, 1, c, at_x)
    load_caption.wait()
    txt[pl.ds(0, rows), :] = unit_rows(caption_ref[...])[0].astype(BF16)
    for c in range(Z_AHEAD):
        start_txt_z(c)
    for c in every:
        txt_y[0, c] = send(txt, 0, txt, 1, c, at_y)
    txt_c[0] = send(txt, 0, txt, 2, None, at_core)

    multiplier, offset = multiplier_ref[0], offset_ref[0]
    tile = 2 * rows

    def sigmoid_tile(lines, columns):
        energies = lax.dot_general(
            img[lines, :], txt[columns, :], (((1,), (1,)), ((), ())), preferred_element_type=F32
        )
        return 1.0 / (1.0 + jnp.exp(-(multiplier * energies + offset)))

    def near_tiles():
        lines, columns = pl.ds(0, tile), pl.ds(0, 2 * tile)
        values = sigmoid_tile(lines, columns)
        same = lax.broadcasted_iota(jnp.int32, values.shape, 0) == lax.broadcasted_iota(
            jnp.int32, values.shape, 1
        )
        same = same & (lax.broadcasted_iota(jnp.int32, values.shape, 0) < rows)
        coup[lines, columns] = (values - jnp.where(same, 1.0, 0.0)).astype(BF16)

    for c in every:
        for d in range(1, far):
            img_z[d, c].wait_recv()
            img_x[d, c] = send(img, 2 * (far - d), img, 2 * (far - d) + 1, c, at_x)
        if c + Z_AHEAD < CHUNKS:
            start_img_z(c + Z_AHEAD)
        txt_z[c].wait_recv()
        txt_y[1, c] = send(txt, 4, txt, 5, c, at_y)
        if c + Z_AHEAD < CHUNKS:
            start_txt_z(c + Z_AHEAD)
        txt_c[2, c] = send(txt, 4, txt, 6, c, at_core)
        if c == 0:
            for e in every:
                txt_y[0, e].wait_recv()
            txt_c[1] = send(txt, 1, txt, 3, None, at_core)
            for e in every:
                img_x[0, e].wait_recv()
            txt_c[0].wait_recv()
            txt_c[1].wait_recv()
            near_tiles()
    for c in every:
        txt_y[1, c].wait_recv()
        txt_c[3, c] = send(txt, 5, txt, 7, c, at_core)
    for c in every:
        for d in range(1, far):
            img_x[d, c].wait_recv()
        txt_c[2, c].wait_recv()
        txt_c[3, c].wait_recv()

    def image_part(step):
        lines = pl.ds(pl.multiple_of(step * tile, tile), tile)
        total = jnp.dot(coup[lines, :], txt[...], preferred_element_type=F32)
        here = pl.ds(pl.multiple_of(step * rows, rows), rows)
        d_img[here, :] = total[:rows]
        send_x[here, :] = total[rows:].astype(BF16)

    def far_tiles(step):
        lines = pl.ds(pl.multiple_of(step * tile, tile), tile)
        coup[lines, :] = sigmoid_tile(lines, slice(None)).astype(BF16)
        image_part(step)

    def text_part(slot):
        return lax.dot_general(
            coup[:, pl.ds(slot * rows, tile)],
            img[...],
            (((0,), (0,)), ((), ())),
            preferred_element_type=F32,
        )

    grad_c, grad_x, grad_y, grad_z, grad_w = {}, {}, {}, {}, {}
    order_x = [[(d, c) for d in range(1, far)] for c in every] + [[(0, c)] for c in every]
    order_y = [(1, c) for c in every] + [(0, c) for c in every]

    def start_x(k):
        if k >= AHEAD:
            for key in order_x[k - AHEAD]:
                sent(grad_x[key])
        for d, c in order_x[k]:
            grad_x[d, c] = send(send_x, d, recv_x, d, c, at_x)

    def start_y(k):
        if k >= AHEAD:
            sent(grad_y[order_y[k - AHEAD]])
        dz, c = order_y[k]
        grad_y[dz, c] = send(send_y, dz, recv_y, dz, c, at_y)

    def core_part(dz):
        send_c[pl.ds(2 * dz * rows, tile), :] = text_part(dz * 4 + 2).astype(BF16)
        for dy in (1, 0):
            for c in every:
                grad_c[dz, dy, c] = send(send_c, dz * 2 + dy, recv_c, dz * 2 + dy, c, at_core)

    def own_part(dz):
        d_txt[pl.ds(2 * dz * rows, tile), :] = text_part(dz * 4)

    def y_sum(dz, c):
        grad_c[dz, 1, c].wait_recv()
        mine = pl.ds((2 * dz + 1) * rows + c * part, part)
        send_y[pl.ds(dz * rows + c * part, part), :] = (
            d_txt[mine, :] + recv_c[mine, :].astype(F32)
        ).astype(BF16)

    def forward_z(c):
        for d in range(1, far):
            grad_x[d, c].wait_recv()
            mine = pl.ds(d * rows + c * part, part)
            send_z[mine, :] = (d_img[mine, :] + recv_x[mine, :].astype(F32)).astype(BF16)
            grad_z[d, c] = send(send_z, d, recv_z, far - d, c, at_far[d])

    def forward_near(c):
        grad_c[1, 0, c].wait_recv()
        grad_y[1, c].wait_recv()
        mine = pl.ds(2 * rows + c * part, part)
        here = pl.ds(c * part, part)
        send_w[here, :] = (
            d_txt[mine, :]
            + recv_c[mine, :].astype(F32)
            + recv_y[pl.ds(rows + c * part, part), :].astype(F32)
        ).astype(BF16)
        grad_w[c] = send(send_w, 0, recv_w, 0, c, at_near)

    for_tiles(1, far, far_tiles)
    for c in every:
        start_x(c)
    lines, columns = pl.ds(0, tile), pl.ds(2 * tile, 2 * tile)
    coup[lines, columns] = sigmoid_tile(lines, columns).astype(BF16)
    core_part(1)
    own_part(1)
    for c in every:
        y_sum(1, c)
        start_y(c)
    image_part(0)
    for c in range(CHUNKS // 2):
        forward_z(c)
        start_x(CHUNKS + c)
    core_part(0)
    for c in range(CHUNKS // 2, CHUNKS):
        forward_z(c)
        start_x(CHUNKS + c)
    own_part(0)
    for c in every:
        y_sum(0, c)
        start_y(CHUNKS + c)
        forward_near(c)

    samples = rows * pairs
    derivative = adjoint_ref[0] * multiplier / samples
    for c in every:
        here = pl.ds(c * part, part)
        grad_x[0, c].wait_recv()
        total = d_img[here, :] + recv_x[here, :].astype(F32)
        for d in range(1, far):
            grad_z[d, c].wait_recv()
            total += recv_z[pl.ds((far - d) * rows + c * part, part), :].astype(F32)
        unit, scale = unit_rows(picture_ref[here, :])
        image_grad_ref[here, :] = unit_grad(unit, scale, derivative * total)
        grad_c[0, 0, c].wait_recv()
        grad_y[0, c].wait_recv()
        grad_w[c].wait_recv()
        total = (
            d_txt[here, :]
            + recv_c[here, :].astype(F32)
            + recv_y[here, :].astype(F32)
            + recv_w[here, :].astype(F32)
        )
        unit, scale = unit_rows(caption_ref[here, :])
        text_grad_ref[here, :] = unit_grad(unit, scale, derivative * total)
    for copy in started.values():
        if copy is not None:
            copy.wait_send()


def on_device(far, pairs, picture, caption, multiplier, offset, adjoint):
    rows, width = picture.shape
    copies = CHUNKS * (4 * far + 12)
    vmem = pl.BlockSpec(memory_space=pltpu.VMEM)
    hbm = pl.BlockSpec(memory_space=pltpu.HBM)
    smem = pl.BlockSpec(memory_space=pltpu.SMEM)

    def slots(count, kind=BF16):
        return pltpu.VMEM((count * rows, width), kind)

    out = jax.ShapeDtypeStruct((rows, width), F32)
    grads = pl.pallas_call(
        functools.partial(kernel, far, pairs),
        out_shape=(out, out),
        in_specs=[hbm, hbm, smem, smem, smem],
        out_specs=(vmem, vmem),
        scratch_shapes=[
            slots(1),
            slots(1),
            slots(2 * far),
            slots(8),
            pltpu.VMEM((2 * far * rows, 8 * rows), BF16),
            slots(far, F32),
            slots(4, F32),
            slots(far),
            slots(far),
            slots(far),
            slots(far),
            slots(4),
            slots(4),
            slots(2),
            slots(2),
            slots(1),
            slots(1),
            pltpu.SemaphoreType.DMA((2,)),
            pltpu.SemaphoreType.DMA((copies,)),
            pltpu.SemaphoreType.DMA((copies,)),
        ],
        compiler_params=pltpu.CompilerParams(
            collective_id=0, has_side_effects=True, vmem_limit_bytes=52 * 1024 * 1024
        ),
    )(
        pltpu.with_memory_space_constraint(picture, pltpu.HBM),
        pltpu.with_memory_space_constraint(caption, pltpu.HBM),
        multiplier,
        offset,
        adjoint,
    )
    return copied_out(*grads)


def copy_out_kernel(image_ref, text_ref, image_out, text_out, sem):
    copies = [
        pltpu.make_async_copy(image_ref, image_out, sem.at[0]),
        pltpu.make_async_copy(text_ref, text_out, sem.at[1]),
    ]
    for copy in copies:
        copy.start()
    for copy in copies:
        copy.wait()


def copied_out(image_grad, text_grad):
    hbm = pl.BlockSpec(memory_space=pltpu.HBM)
    anywhere = pl.BlockSpec(memory_space=pl.ANY)
    return pl.pallas_call(
        copy_out_kernel,
        out_shape=(
            jax.ShapeDtypeStruct(image_grad.shape, F32),
            jax.ShapeDtypeStruct(text_grad.shape, F32),
        ),
        in_specs=[anywhere, anywhere],
        out_specs=(hbm, hbm),
        scratch_shapes=[pltpu.SemaphoreType.DMA((2,))],
        compiler_params=pltpu.CompilerParams(vmem_limit_bytes=4 * 1024 * 1024),
    )(image_grad, text_grad)


def solution(mesh):
    placed = (P(("blk", "grp"), None), P(("blk", "grp"), None), P(), P(), P())
    pairs = mesh.shape["blk"] * mesh.shape["grp"]
    far = mesh.shape["grp"] // 4
    return jax.shard_map(
        functools.partial(on_device, far, pairs),
        mesh=mesh,
        in_specs=placed,
        out_specs=(P(("blk", "grp"), None), P(("blk", "grp"), None)),
        check_vma=False,
    )
```

```python
import functools
import math

import jax
import jax.numpy as jnp
from jax import lax
from jax.experimental import pallas as pl
from jax.experimental.pallas import tpu as pltpu
from jax.sharding import PartitionSpec as P

MESH = pl.DeviceIdType.MESH
CHUNKS = 2
AHEAD = 2
BF16 = jnp.bfloat16
F32 = jnp.float32


def unit_rows(embedding):
    values = embedding.astype(F32)
    row_scale = lax.rsqrt(jnp.mean(values * values, axis=1, keepdims=True) + 1e-06) / math.sqrt(
        values.shape[1]
    )
    return (values * row_scale, row_scale)


def unit_grad(unit_vals, row_scale, upstream_grad):
    return row_scale * (
        upstream_grad - unit_vals * jnp.sum(unit_vals * upstream_grad, axis=1, keepdims=True)
    )


def for_tiles(first, end, body):
    if end - first == 1:
        body(first)
    else:

        @pl.loop(first, end)
        def _(step):
            body(step)


def kernel(
    far,
    pairs,
    picture_hbm,
    caption_hbm,
    multiplier_ref,
    offset_ref,
    adjoint_ref,
    image_grad_ref,
    text_grad_ref,
    picture_ref,
    caption_ref,
    img,
    txt,
    coup,
    d_img,
    d_txt,
    send_x,
    recv_x,
    send_z,
    recv_z,
    send_c,
    recv_c,
    send_y,
    recv_y,
    send_w,
    recv_w,
    load_sem,
    send_sem,
    recv_sem,
):
    rows = picture_ref.shape[0]
    part = rows // CHUNKS
    load_picture = pltpu.make_async_copy(picture_hbm, picture_ref, load_sem.at[0])
    load_caption = pltpu.make_async_copy(caption_hbm, caption_ref, load_sem.at[1])
    load_picture.start()
    load_caption.start()
    blk, grp = lax.axis_index("blk"), lax.axis_index("grp")
    y, core = lax.div(blk, 2), lax.rem(blk, 2)
    h, near, x = lax.div(grp, 4), lax.rem(lax.div(grp, 2), 2), lax.rem(grp, 2)
    at_x = (blk, h * 4 + near * 2 + (1 - x))
    at_near = (blk, h * 4 + (1 - near) * 2 + x)
    at_y = ((1 - y) * 2 + core, grp)
    at_core = (y * 2 + (1 - core), grp)
    at_far = [None] + [
        (blk, lax.rem(h + d, far) * 4 + near * 2 + x) for d in range(1, far)
    ]

    barrier = pltpu.get_barrier_semaphore()
    for peer in [at_x, at_near, at_y, at_core] + at_far[1:]:
        pl.semaphore_signal(barrier, inc=1, device_id=peer, device_id_type=MESH)

    started = {}

    def send(src, src_slot, dst, dst_slot, chunk, peer):
        number = len(started)
        first, length = (0, rows) if chunk is None else (chunk * part, part)
        copy = pltpu.make_async_remote_copy(
            src_ref=src.at[pl.ds(src_slot * rows + first, length), :],
            dst_ref=dst.at[pl.ds(dst_slot * rows + first, length), :],
            send_sem=send_sem.at[number],
            recv_sem=recv_sem.at[number],
            device_id=peer,
            device_id_type=MESH,
        )
        copy.start()
        started[number] = copy
        return copy

    def sent(copy):
        copy.wait_send()
        for number in started:
            if started[number] is copy:
                started[number] = None

    every = range(CHUNKS)
    img_z, txt_z, img_x, txt_y, txt_c = {}, {}, {}, {}, {}

    load_picture.wait()
    img[pl.ds(0, rows), :] = unit_rows(picture_ref[...])[0].astype(BF16)
    pl.semaphore_wait(barrier, 3 + far)
    for c in every:
        for d in range(1, far):
            img_z[d, c] = send(img, 0, img, 2 * (far - d), c, at_far[d])
        img_x[0, c] = send(img, 0, img, 1, c, at_x)
    load_caption.wait()
    txt[pl.ds(0, rows), :] = unit_rows(caption_ref[...])[0].astype(BF16)
    for c in every:
        txt_z[c] = send(txt, 0, txt, 4, c, at_near)
        txt_y[0, c] = send(txt, 0, txt, 1, c, at_y)
    txt_c[0] = send(txt, 0, txt, 2, None, at_core)

    multiplier, offset = multiplier_ref[0], offset_ref[0]
    tile = 2 * rows

    def sigmoid_tile(lines, columns):
        energies = lax.dot_general(
            img[lines, :], txt[columns, :], (((1,), (1,)), ((), ())), preferred_element_type=F32
        )
        return 1.0 / (1.0 + jnp.exp(-(multiplier * energies + offset)))

    def near_tiles():
        lines, columns = pl.ds(0, tile), pl.ds(0, 2 * tile)
        values = sigmoid_tile(lines, columns)
        same = lax.broadcasted_iota(jnp.int32, values.shape, 0) == lax.broadcasted_iota(
            jnp.int32, values.shape, 1
        )
        same = same & (lax.broadcasted_iota(jnp.int32, values.shape, 0) < rows)
        coup[lines, columns] = (values - jnp.where(same, 1.0, 0.0)).astype(BF16)

    for c in every:
        txt_y[0, c].wait_recv()
    txt_c[1] = send(txt, 1, txt, 3, None, at_core)
    for c in every:
        img_x[0, c].wait_recv()
    txt_c[0].wait_recv()
    txt_c[1].wait_recv()
    near_tiles()
    for c in every:
        for d in range(1, far):
            img_z[d, c].wait_recv()
            img_x[d, c] = send(img, 2 * (far - d), img, 2 * (far - d) + 1, c, at_x)
        txt_z[c].wait_recv()
        txt_y[1, c] = send(txt, 4, txt, 5, c, at_y)
    txt_c[2] = send(txt, 4, txt, 6, None, at_core)
    for c in every:
        txt_y[1, c].wait_recv()
        txt_c[3, c] = send(txt, 5, txt, 7, c, at_core)
    for c in every:
        for d in range(1, far):
            img_x[d, c].wait_recv()

    def far_near_tiles(step):
        lines = pl.ds(pl.multiple_of(step * tile, tile), tile)
        columns = pl.ds(0, 2 * tile)
        coup[lines, columns] = sigmoid_tile(lines, columns).astype(BF16)

    for_tiles(1, far, far_near_tiles)
    txt_c[2].wait_recv()
    for c in every:
        txt_c[3, c].wait_recv()

    def image_part(step):
        lines = pl.ds(pl.multiple_of(step * tile, tile), tile)
        total = jnp.dot(coup[lines, :], txt[...], preferred_element_type=F32)
        here = pl.ds(pl.multiple_of(step * rows, rows), rows)
        d_img[here, :] = total[:rows]
        send_x[here, :] = total[rows:].astype(BF16)

    def far_tiles(step):
        lines = pl.ds(pl.multiple_of(step * tile, tile), tile)
        columns = pl.ds(2 * tile, 2 * tile)
        coup[lines, columns] = sigmoid_tile(lines, columns).astype(BF16)
        image_part(step)

    def text_part(slot):
        return lax.dot_general(
            coup[:, pl.ds(slot * rows, tile)],
            img[...],
            (((0,), (0,)), ((), ())),
            preferred_element_type=F32,
        )

    grad_c, grad_x, grad_y, grad_z, grad_w = {}, {}, {}, {}, {}
    order_x = [[(d, c) for d in range(1, far)] for c in every] + [[(0, c)] for c in every]
    order_y = [(1, c) for c in every] + [(0, c) for c in every]

    def start_x(k):
        if k >= AHEAD:
            for key in order_x[k - AHEAD]:
                sent(grad_x[key])
        for d, c in order_x[k]:
            grad_x[d, c] = send(send_x, d, recv_x, d, c, at_x)

    def start_y(k):
        if k >= AHEAD:
            sent(grad_y[order_y[k - AHEAD]])
        dz, c = order_y[k]
        grad_y[dz, c] = send(send_y, dz, recv_y, dz, c, at_y)

    def core_part(dz):
        send_c[pl.ds(2 * dz * rows, tile), :] = text_part(dz * 4 + 2).astype(BF16)
        for dy in (1, 0):
            grad_c[dz, dy] = send(send_c, dz * 2 + dy, recv_c, dz * 2 + dy, None, at_core)

    def own_part(dz):
        d_txt[pl.ds(2 * dz * rows, tile), :] = text_part(dz * 4)

    def y_sum(dz, c):
        if c == 0:
            grad_c[dz, 1].wait_recv()
        mine = pl.ds((2 * dz + 1) * rows + c * part, part)
        send_y[pl.ds(dz * rows + c * part, part), :] = (
            d_txt[mine, :] + recv_c[mine, :].astype(F32)
        ).astype(BF16)

    def forward_z(c):
        for d in range(1, far):
            grad_x[d, c].wait_recv()
            mine = pl.ds(d * rows + c * part, part)
            send_z[mine, :] = (d_img[mine, :] + recv_x[mine, :].astype(F32)).astype(BF16)
            grad_z[d, c] = send(send_z, d, recv_z, far - d, c, at_far[d])

    def forward_near(c):
        if c == 0:
            grad_c[1, 0].wait_recv()
        grad_y[1, c].wait_recv()
        mine = pl.ds(2 * rows + c * part, part)
        here = pl.ds(c * part, part)
        send_w[here, :] = (
            d_txt[mine, :]
            + recv_c[mine, :].astype(F32)
            + recv_y[pl.ds(rows + c * part, part), :].astype(F32)
        ).astype(BF16)
        grad_w[c] = send(send_w, 0, recv_w, 0, c, at_near)

    for_tiles(1, far, far_tiles)
    for c in every:
        start_x(c)
    lines, columns = pl.ds(0, tile), pl.ds(2 * tile, 2 * tile)
    coup[lines, columns] = sigmoid_tile(lines, columns).astype(BF16)
    core_part(1)
    own_part(1)
    for c in every:
        y_sum(1, c)
        start_y(c)
    image_part(0)
    for c in range(CHUNKS // 2):
        forward_z(c)
        start_x(CHUNKS + c)
    core_part(0)
    for c in range(CHUNKS // 2, CHUNKS):
        forward_z(c)
        start_x(CHUNKS + c)
    own_part(0)
    for c in every:
        y_sum(0, c)
        start_y(CHUNKS + c)
        forward_near(c)

    samples = rows * pairs
    derivative = adjoint_ref[0] * multiplier / samples
    for c in every:
        here = pl.ds(c * part, part)
        grad_x[0, c].wait_recv()
        total = d_img[here, :] + recv_x[here, :].astype(F32)
        for d in range(1, far):
            grad_z[d, c].wait_recv()
            total += recv_z[pl.ds((far - d) * rows + c * part, part), :].astype(F32)
        unit, scale = unit_rows(picture_ref[here, :])
        image_grad_ref[here, :] = unit_grad(unit, scale, derivative * total)
        if c == 0:
            grad_c[0, 0].wait_recv()
        grad_y[0, c].wait_recv()
        grad_w[c].wait_recv()
        total = (
            d_txt[here, :]
            + recv_c[here, :].astype(F32)
            + recv_y[here, :].astype(F32)
            + recv_w[here, :].astype(F32)
        )
        unit, scale = unit_rows(caption_ref[here, :])
        text_grad_ref[here, :] = unit_grad(unit, scale, derivative * total)
    for copy in started.values():
        if copy is not None:
            copy.wait_send()


def on_device(far, pairs, picture, caption, multiplier, offset, adjoint):
    rows, width = picture.shape
    copies = CHUNKS * (4 * far + 12)
    vmem = pl.BlockSpec(memory_space=pltpu.VMEM)
    hbm = pl.BlockSpec(memory_space=pltpu.HBM)
    smem = pl.BlockSpec(memory_space=pltpu.SMEM)

    def slots(count, kind=BF16):
        return pltpu.VMEM((count * rows, width), kind)

    out = jax.ShapeDtypeStruct((rows, width), F32)
    grads = pl.pallas_call(
        functools.partial(kernel, far, pairs),
        out_shape=(out, out),
        in_specs=[hbm, hbm, smem, smem, smem],
        out_specs=(vmem, vmem),
        scratch_shapes=[
            slots(1),
            slots(1),
            slots(2 * far),
            slots(8),
            pltpu.VMEM((2 * far * rows, 8 * rows), BF16),
            slots(far, F32),
            slots(4, F32),
            slots(far),
            slots(far),
            slots(far),
            slots(far),
            slots(4),
            slots(4),
            slots(2),
            slots(2),
            slots(1),
            slots(1),
            pltpu.SemaphoreType.DMA((2,)),
            pltpu.SemaphoreType.DMA((copies,)),
            pltpu.SemaphoreType.DMA((copies,)),
        ],
        compiler_params=pltpu.CompilerParams(
            collective_id=0, has_side_effects=True, vmem_limit_bytes=52 * 1024 * 1024
        ),
    )(
        pltpu.with_memory_space_constraint(picture, pltpu.HBM),
        pltpu.with_memory_space_constraint(caption, pltpu.HBM),
        multiplier,
        offset,
        adjoint,
    )
    return copied_out(*grads)


def copy_out_kernel(image_ref, text_ref, image_out, text_out, sem):
    copies = [
        pltpu.make_async_copy(image_ref, image_out, sem.at[0]),
        pltpu.make_async_copy(text_ref, text_out, sem.at[1]),
    ]
    for copy in copies:
        copy.start()
    for copy in copies:
        copy.wait()


def copied_out(image_grad, text_grad):
    hbm = pl.BlockSpec(memory_space=pltpu.HBM)
    anywhere = pl.BlockSpec(memory_space=pl.ANY)
    return pl.pallas_call(
        copy_out_kernel,
        out_shape=(
            jax.ShapeDtypeStruct(image_grad.shape, F32),
            jax.ShapeDtypeStruct(text_grad.shape, F32),
        ),
        in_specs=[anywhere, anywhere],
        out_specs=(hbm, hbm),
        scratch_shapes=[pltpu.SemaphoreType.DMA((2,))],
        compiler_params=pltpu.CompilerParams(vmem_limit_bytes=4 * 1024 * 1024),
    )(image_grad, text_grad)


def solution(mesh):
    placed = (P(("blk", "grp"), None), P(("blk", "grp"), None), P(), P(), P())
    pairs = mesh.shape["blk"] * mesh.shape["grp"]
    far = mesh.shape["grp"] // 4
    return jax.shard_map(
        functools.partial(on_device, far, pairs),
        mesh=mesh,
        in_specs=placed,
        out_specs=(P(("blk", "grp"), None), P(("blk", "grp"), None)),
        check_vma=False,
    )
```

```python
import functools
import math

import jax
import jax.numpy as jnp
from jax import lax
from jax.experimental import pallas as pl
from jax.experimental.pallas import tpu as pltpu
from jax.sharding import PartitionSpec as P

MESH = pl.DeviceIdType.MESH
CHUNKS = 2
AHEAD = 2
Z_AHEAD = 2
BF16 = jnp.bfloat16
F32 = jnp.float32


def unit_rows(embedding):
    values = embedding.astype(F32)
    row_scale = lax.rsqrt(jnp.mean(values * values, axis=1, keepdims=True) + 1e-06) / math.sqrt(
        values.shape[1]
    )
    return (values * row_scale, row_scale)


def unit_grad(unit_vals, row_scale, upstream_grad):
    return row_scale * (
        upstream_grad - unit_vals * jnp.sum(unit_vals * upstream_grad, axis=1, keepdims=True)
    )


def for_tiles(first, end, body):
    if end - first == 1:
        body(first)
    else:

        @pl.loop(first, end)
        def _(step):
            body(step)


def kernel(
    far,
    pairs,
    picture_hbm,
    caption_hbm,
    multiplier_ref,
    offset_ref,
    adjoint_ref,
    image_grad_ref,
    text_grad_ref,
    picture_ref,
    caption_ref,
    img,
    txt,
    coup,
    d_img,
    d_txt,
    send_x,
    recv_x,
    send_z,
    recv_z,
    send_c,
    recv_c,
    send_y,
    recv_y,
    send_w,
    recv_w,
    load_sem,
    send_sem,
    recv_sem,
):
    rows = picture_ref.shape[0]
    part = rows // CHUNKS
    load_picture = pltpu.make_async_copy(picture_hbm, picture_ref, load_sem.at[0])
    load_caption = pltpu.make_async_copy(caption_hbm, caption_ref, load_sem.at[1])
    load_picture.start()
    load_caption.start()
    blk, grp = lax.axis_index("blk"), lax.axis_index("grp")
    y, core = lax.div(blk, 2), lax.rem(blk, 2)
    h, near, x = lax.div(grp, 4), lax.rem(lax.div(grp, 2), 2), lax.rem(grp, 2)
    at_x = (blk, h * 4 + near * 2 + (1 - x))
    at_near = (blk, h * 4 + (1 - near) * 2 + x)
    at_y = ((1 - y) * 2 + core, grp)
    at_core = (y * 2 + (1 - core), grp)
    at_far = [None] + [
        (blk, lax.rem(h + d, far) * 4 + near * 2 + x) for d in range(1, far)
    ]

    barrier = pltpu.get_barrier_semaphore()
    for peer in [at_x, at_near, at_y, at_core] + at_far[1:]:
        pl.semaphore_signal(barrier, inc=1, device_id=peer, device_id_type=MESH)

    load_picture.wait()
    img[pl.ds(0, rows), :] = unit_rows(picture_ref[...])[0].astype(BF16)
    load_caption.wait()
    txt[pl.ds(0, rows), :] = unit_rows(caption_ref[...])[0].astype(BF16)
    pl.semaphore_wait(barrier, 3 + far)

    started = {}

    def send(src, src_slot, dst, dst_slot, chunk, peer):
        number = len(started)
        copy = pltpu.make_async_remote_copy(
            src_ref=src.at[pl.ds(src_slot * rows + chunk * part, part), :],
            dst_ref=dst.at[pl.ds(dst_slot * rows + chunk * part, part), :],
            send_sem=send_sem.at[number],
            recv_sem=recv_sem.at[number],
            device_id=peer,
            device_id_type=MESH,
        )
        copy.start()
        started[number] = copy
        return copy

    def sent(copy):
        copy.wait_send()
        for number in started:
            if started[number] is copy:
                started[number] = None

    every = range(CHUNKS)
    img_z, txt_z, img_x, txt_y, txt_c = {}, {}, {}, {}, {}

    def start_z(c):
        for d in range(1, far):
            if c >= Z_AHEAD:
                sent(img_z[d, c - Z_AHEAD])
            img_z[d, c] = send(img, 0, img, 2 * (far - d), c, at_far[d])
        if c >= Z_AHEAD:
            sent(txt_z[c - Z_AHEAD])
        txt_z[c] = send(txt, 0, txt, 4, c, at_near)

    for c in range(Z_AHEAD):
        start_z(c)
    for c in every:
        img_x[0, c] = send(img, 0, img, 1, c, at_x)
        txt_y[0, c] = send(txt, 0, txt, 1, c, at_y)
    for c in every:
        txt_c[0, c] = send(txt, 0, txt, 2, c, at_core)

    multiplier, offset = multiplier_ref[0], offset_ref[0]
    tile = 2 * rows

    def sigmoid_tile(lines, columns):
        energies = lax.dot_general(
            img[lines, :], txt[columns, :], (((1,), (1,)), ((), ())), preferred_element_type=F32
        )
        return 1.0 / (1.0 + jnp.exp(-(multiplier * energies + offset)))

    def near_tiles():
        lines, columns = pl.ds(0, tile), pl.ds(0, 2 * tile)
        values = sigmoid_tile(lines, columns)
        same = lax.broadcasted_iota(jnp.int32, values.shape, 0) == lax.broadcasted_iota(
            jnp.int32, values.shape, 1
        )
        same = same & (lax.broadcasted_iota(jnp.int32, values.shape, 0) < rows)
        coup[lines, columns] = (values - jnp.where(same, 1.0, 0.0)).astype(BF16)

    for c in every:
        if c + Z_AHEAD < CHUNKS:
            start_z(c + Z_AHEAD)
        for d in range(1, far):
            img_z[d, c].wait_recv()
            img_x[d, c] = send(img, 2 * (far - d), img, 2 * (far - d) + 1, c, at_x)
        txt_z[c].wait_recv()
        txt_y[1, c] = send(txt, 4, txt, 5, c, at_y)
        txt_c[2, c] = send(txt, 4, txt, 6, c, at_core)
        if c == CHUNKS // 2:
            for e in every:
                txt_y[0, e].wait_recv()
                txt_c[1, e] = send(txt, 1, txt, 3, e, at_core)
    for c in every:
        txt_y[1, c].wait_recv()
        txt_c[3, c] = send(txt, 5, txt, 7, c, at_core)
    for c in every:
        img_x[0, c].wait_recv()
        txt_c[0, c].wait_recv()
        txt_c[1, c].wait_recv()
    near_tiles()
    for c in every:
        for d in range(1, far):
            img_x[d, c].wait_recv()

    def far_near_tiles(step):
        lines = pl.ds(pl.multiple_of(step * tile, tile), tile)
        columns = pl.ds(0, 2 * tile)
        coup[lines, columns] = sigmoid_tile(lines, columns).astype(BF16)

    for_tiles(1, far, far_near_tiles)
    for c in every:
        txt_c[2, c].wait_recv()
        txt_c[3, c].wait_recv()

    def image_part(step):
        lines = pl.ds(pl.multiple_of(step * tile, tile), tile)
        total = jnp.dot(coup[lines, :], txt[...], preferred_element_type=F32)
        here = pl.ds(pl.multiple_of(step * rows, rows), rows)
        d_img[here, :] = total[:rows]
        send_x[here, :] = total[rows:].astype(BF16)

    def far_tiles(step):
        lines = pl.ds(pl.multiple_of(step * tile, tile), tile)
        columns = pl.ds(2 * tile, 2 * tile)
        coup[lines, columns] = sigmoid_tile(lines, columns).astype(BF16)
        image_part(step)

    def text_part(slot):
        return lax.dot_general(
            coup[:, pl.ds(slot * rows, tile)],
            img[...],
            (((0,), (0,)), ((), ())),
            preferred_element_type=F32,
        )

    grad_c, grad_x, grad_y, grad_z, grad_w = {}, {}, {}, {}, {}
    order_x = [[(d, c) for d in range(1, far)] for c in every] + [[(0, c)] for c in every]
    order_y = [(1, c) for c in every] + [(0, c) for c in every]

    def start_x(k):
        if k >= AHEAD:
            for key in order_x[k - AHEAD]:
                sent(grad_x[key])
        for d, c in order_x[k]:
            grad_x[d, c] = send(send_x, d, recv_x, d, c, at_x)

    def start_y(k):
        if k >= AHEAD:
            sent(grad_y[order_y[k - AHEAD]])
        dz, c = order_y[k]
        grad_y[dz, c] = send(send_y, dz, recv_y, dz, c, at_y)

    def core_part(dz):
        send_c[pl.ds(2 * dz * rows, tile), :] = text_part(dz * 4 + 2).astype(BF16)
        for dy in (1, 0):
            for c in every:
                grad_c[dz, dy, c] = send(send_c, dz * 2 + dy, recv_c, dz * 2 + dy, c, at_core)

    def own_part(dz):
        d_txt[pl.ds(2 * dz * rows, tile), :] = text_part(dz * 4)

    def y_sum(dz, c):
        grad_c[dz, 1, c].wait_recv()
        mine = pl.ds((2 * dz + 1) * rows + c * part, part)
        send_y[pl.ds(dz * rows + c * part, part), :] = (
            d_txt[mine, :] + recv_c[mine, :].astype(F32)
        ).astype(BF16)

    def forward_z(c):
        for d in range(1, far):
            grad_x[d, c].wait_recv()
            mine = pl.ds(d * rows + c * part, part)
            send_z[mine, :] = (d_img[mine, :] + recv_x[mine, :].astype(F32)).astype(BF16)
            grad_z[d, c] = send(send_z, d, recv_z, far - d, c, at_far[d])

    def forward_near(c):
        grad_c[1, 0, c].wait_recv()
        grad_y[1, c].wait_recv()
        mine = pl.ds(2 * rows + c * part, part)
        here = pl.ds(c * part, part)
        send_w[here, :] = (
            d_txt[mine, :]
            + recv_c[mine, :].astype(F32)
            + recv_y[pl.ds(rows + c * part, part), :].astype(F32)
        ).astype(BF16)
        grad_w[c] = send(send_w, 0, recv_w, 0, c, at_near)

    for_tiles(1, far, far_tiles)
    for c in every:
        start_x(c)
    lines, columns = pl.ds(0, tile), pl.ds(2 * tile, 2 * tile)
    coup[lines, columns] = sigmoid_tile(lines, columns).astype(BF16)
    core_part(1)
    own_part(1)
    for c in every:
        y_sum(1, c)
        start_y(c)
    image_part(0)
    for c in range(CHUNKS // 2):
        forward_z(c)
        start_x(CHUNKS + c)
    core_part(0)
    for c in range(CHUNKS // 2, CHUNKS):
        forward_z(c)
        start_x(CHUNKS + c)
    own_part(0)
    for c in every:
        y_sum(0, c)
        start_y(CHUNKS + c)
        forward_near(c)

    samples = rows * pairs
    derivative = adjoint_ref[0] * multiplier / samples
    for c in every:
        here = pl.ds(c * part, part)
        grad_x[0, c].wait_recv()
        total = d_img[here, :] + recv_x[here, :].astype(F32)
        for d in range(1, far):
            grad_z[d, c].wait_recv()
            total += recv_z[pl.ds((far - d) * rows + c * part, part), :].astype(F32)
        unit, scale = unit_rows(picture_ref[here, :])
        image_grad_ref[here, :] = unit_grad(unit, scale, derivative * total)
        grad_c[0, 0, c].wait_recv()
        grad_y[0, c].wait_recv()
        grad_w[c].wait_recv()
        total = (
            d_txt[here, :]
            + recv_c[here, :].astype(F32)
            + recv_y[here, :].astype(F32)
            + recv_w[here, :].astype(F32)
        )
        unit, scale = unit_rows(caption_ref[here, :])
        text_grad_ref[here, :] = unit_grad(unit, scale, derivative * total)
    for copy in started.values():
        if copy is not None:
            copy.wait_send()


def on_device(far, pairs, picture, caption, multiplier, offset, adjoint):
    rows, width = picture.shape
    copies = CHUNKS * (4 * far + 12)
    vmem = pl.BlockSpec(memory_space=pltpu.VMEM)
    hbm = pl.BlockSpec(memory_space=pltpu.HBM)
    smem = pl.BlockSpec(memory_space=pltpu.SMEM)

    def slots(count, kind=BF16):
        return pltpu.VMEM((count * rows, width), kind)

    out = jax.ShapeDtypeStruct((rows, width), F32)
    grads = pl.pallas_call(
        functools.partial(kernel, far, pairs),
        out_shape=(out, out),
        in_specs=[hbm, hbm, smem, smem, smem],
        out_specs=(vmem, vmem),
        scratch_shapes=[
            slots(1),
            slots(1),
            slots(2 * far),
            slots(8),
            pltpu.VMEM((2 * far * rows, 8 * rows), BF16),
            slots(far, F32),
            slots(4, F32),
            slots(far),
            slots(far),
            slots(far),
            slots(far),
            slots(4),
            slots(4),
            slots(2),
            slots(2),
            slots(1),
            slots(1),
            pltpu.SemaphoreType.DMA((2,)),
            pltpu.SemaphoreType.DMA((copies,)),
            pltpu.SemaphoreType.DMA((copies,)),
        ],
        compiler_params=pltpu.CompilerParams(
            collective_id=0, has_side_effects=True, vmem_limit_bytes=52 * 1024 * 1024
        ),
    )(
        pltpu.with_memory_space_constraint(picture, pltpu.HBM),
        pltpu.with_memory_space_constraint(caption, pltpu.HBM),
        multiplier,
        offset,
        adjoint,
    )
    return copied_out(*grads)


def copy_out_kernel(image_ref, text_ref, image_out, text_out, sem):
    copies = [
        pltpu.make_async_copy(image_ref, image_out, sem.at[0]),
        pltpu.make_async_copy(text_ref, text_out, sem.at[1]),
    ]
    for copy in copies:
        copy.start()
    for copy in copies:
        copy.wait()


def copied_out(image_grad, text_grad):
    hbm = pl.BlockSpec(memory_space=pltpu.HBM)
    anywhere = pl.BlockSpec(memory_space=pl.ANY)
    return pl.pallas_call(
        copy_out_kernel,
        out_shape=(
            jax.ShapeDtypeStruct(image_grad.shape, F32),
            jax.ShapeDtypeStruct(text_grad.shape, F32),
        ),
        in_specs=[anywhere, anywhere],
        out_specs=(hbm, hbm),
        scratch_shapes=[pltpu.SemaphoreType.DMA((2,))],
        compiler_params=pltpu.CompilerParams(vmem_limit_bytes=4 * 1024 * 1024),
    )(image_grad, text_grad)


def solution(mesh):
    placed = (P(("blk", "grp"), None), P(("blk", "grp"), None), P(), P(), P())
    pairs = mesh.shape["blk"] * mesh.shape["grp"]
    far = mesh.shape["grp"] // 4
    return jax.shard_map(
        functools.partial(on_device, far, pairs),
        mesh=mesh,
        in_specs=placed,
        out_specs=(P(("blk", "grp"), None), P(("blk", "grp"), None)),
        check_vma=False,
    )
```

```python
import functools
import math

import jax
import jax.numpy as jnp
from jax import lax
from jax.experimental import pallas as pl
from jax.experimental.pallas import tpu as pltpu
from jax.sharding import PartitionSpec as P

MESH = pl.DeviceIdType.MESH
CHUNKS = 4
AHEAD = 4
Z_AHEAD = 4
BF16 = jnp.bfloat16
F32 = jnp.float32


def unit_rows(embedding):
    values = embedding.astype(F32)
    row_scale = lax.rsqrt(jnp.mean(values * values, axis=1, keepdims=True) + 1e-06) / math.sqrt(
        values.shape[1]
    )
    return (values * row_scale, row_scale)


def unit_grad(unit_vals, row_scale, upstream_grad):
    return row_scale * (
        upstream_grad - unit_vals * jnp.sum(unit_vals * upstream_grad, axis=1, keepdims=True)
    )


def for_tiles(first, end, body):
    if end - first == 1:
        body(first)
    else:

        @pl.loop(first, end)
        def _(step):
            body(step)


def kernel(
    far,
    pairs,
    picture_hbm,
    caption_hbm,
    multiplier_ref,
    offset_ref,
    adjoint_ref,
    image_grad_ref,
    text_grad_ref,
    picture_ref,
    caption_ref,
    img,
    txt,
    coup,
    d_img,
    d_txt,
    send_x,
    recv_x,
    send_z,
    recv_z,
    send_c,
    recv_c,
    send_y,
    recv_y,
    send_w,
    recv_w,
    load_sem,
    send_sem,
    recv_sem,
):
    rows = picture_ref.shape[0]
    part = rows // CHUNKS
    load_picture = pltpu.make_async_copy(picture_hbm, picture_ref, load_sem.at[0])
    load_caption = pltpu.make_async_copy(caption_hbm, caption_ref, load_sem.at[1])
    load_picture.start()
    load_caption.start()
    blk, grp = lax.axis_index("blk"), lax.axis_index("grp")
    y, core = lax.div(blk, 2), lax.rem(blk, 2)
    h, near, x = lax.div(grp, 4), lax.rem(lax.div(grp, 2), 2), lax.rem(grp, 2)
    at_x = (blk, h * 4 + near * 2 + (1 - x))
    at_near = (blk, h * 4 + (1 - near) * 2 + x)
    at_y = ((1 - y) * 2 + core, grp)
    at_core = (y * 2 + (1 - core), grp)
    at_far = [None] + [
        (blk, lax.rem(h + d, far) * 4 + near * 2 + x) for d in range(1, far)
    ]

    barrier = pltpu.get_barrier_semaphore()
    for peer in [at_x, at_near, at_y, at_core] + at_far[1:]:
        pl.semaphore_signal(barrier, inc=1, device_id=peer, device_id_type=MESH)

    load_picture.wait()
    img[pl.ds(0, rows), :] = unit_rows(picture_ref[...])[0].astype(BF16)
    load_caption.wait()
    txt[pl.ds(0, rows), :] = unit_rows(caption_ref[...])[0].astype(BF16)
    pl.semaphore_wait(barrier, 3 + far)

    started = {}

    def send(src, src_slot, dst, dst_slot, chunk, peer):
        number = len(started)
        copy = pltpu.make_async_remote_copy(
            src_ref=src.at[pl.ds(src_slot * rows + chunk * part, part), :],
            dst_ref=dst.at[pl.ds(dst_slot * rows + chunk * part, part), :],
            send_sem=send_sem.at[number],
            recv_sem=recv_sem.at[number],
            device_id=peer,
            device_id_type=MESH,
        )
        copy.start()
        started[number] = copy
        return copy

    def sent(copy):
        copy.wait_send()
        for number in started:
            if started[number] is copy:
                started[number] = None

    every = range(CHUNKS)
    img_z, txt_z, img_x, txt_y, txt_c = {}, {}, {}, {}, {}

    def start_z(c):
        for d in range(1, far):
            if c >= Z_AHEAD:
                sent(img_z[d, c - Z_AHEAD])
            img_z[d, c] = send(img, 0, img, 2 * (far - d), c, at_far[d])
        if c >= Z_AHEAD:
            sent(txt_z[c - Z_AHEAD])
        txt_z[c] = send(txt, 0, txt, 4, c, at_near)

    for c in range(Z_AHEAD):
        start_z(c)
    for c in every:
        img_x[0, c] = send(img, 0, img, 1, c, at_x)
        txt_y[0, c] = send(txt, 0, txt, 1, c, at_y)
    for c in every:
        txt_c[0, c] = send(txt, 0, txt, 2, c, at_core)

    multiplier, offset = multiplier_ref[0], offset_ref[0]
    tile = 2 * rows

    def sigmoid_tile(lines, columns):
        energies = lax.dot_general(
            img[lines, :], txt[columns, :], (((1,), (1,)), ((), ())), preferred_element_type=F32
        )
        return 1.0 / (1.0 + jnp.exp(-(multiplier * energies + offset)))

    def near_tiles():
        lines, columns = pl.ds(0, tile), pl.ds(0, 2 * tile)
        values = sigmoid_tile(lines, columns)
        same = lax.broadcasted_iota(jnp.int32, values.shape, 0) == lax.broadcasted_iota(
            jnp.int32, values.shape, 1
        )
        same = same & (lax.broadcasted_iota(jnp.int32, values.shape, 0) < rows)
        coup[lines, columns] = (values - jnp.where(same, 1.0, 0.0)).astype(BF16)

    for c in every:
        if c + Z_AHEAD < CHUNKS:
            start_z(c + Z_AHEAD)
        for d in range(1, far):
            img_z[d, c].wait_recv()
            img_x[d, c] = send(img, 2 * (far - d), img, 2 * (far - d) + 1, c, at_x)
        txt_z[c].wait_recv()
        txt_y[1, c] = send(txt, 4, txt, 5, c, at_y)
        txt_c[2, c] = send(txt, 4, txt, 6, c, at_core)
        if c == CHUNKS // 2:
            for e in every:
                txt_y[0, e].wait_recv()
                txt_c[1, e] = send(txt, 1, txt, 3, e, at_core)
    for c in every:
        img_x[0, c].wait_recv()
        txt_c[0, c].wait_recv()
        txt_c[1, c].wait_recv()
    near_tiles()
    for c in every:
        txt_y[1, c].wait_recv()
        txt_c[3, c] = send(txt, 5, txt, 7, c, at_core)
    for c in every:
        for d in range(1, far):
            img_x[d, c].wait_recv()
        txt_c[2, c].wait_recv()
        txt_c[3, c].wait_recv()

    def image_part(step):
        lines = pl.ds(pl.multiple_of(step * tile, tile), tile)
        total = jnp.dot(coup[lines, :], txt[...], preferred_element_type=F32)
        here = pl.ds(pl.multiple_of(step * rows, rows), rows)
        d_img[here, :] = total[:rows]
        send_x[here, :] = total[rows:].astype(BF16)

    def far_tiles(step):
        lines = pl.ds(pl.multiple_of(step * tile, tile), tile)
        coup[lines, :] = sigmoid_tile(lines, slice(None)).astype(BF16)
        image_part(step)

    def text_part(slot):
        return lax.dot_general(
            coup[:, pl.ds(slot * rows, tile)],
            img[...],
            (((0,), (0,)), ((), ())),
            preferred_element_type=F32,
        )

    grad_c, grad_x, grad_y, grad_z, grad_w = {}, {}, {}, {}, {}
    order_x = [[(d, c) for d in range(1, far)] for c in every] + [[(0, c)] for c in every]
    order_y = [(1, c) for c in every] + [(0, c) for c in every]

    def start_x(k):
        if k >= AHEAD:
            for key in order_x[k - AHEAD]:
                sent(grad_x[key])
        for d, c in order_x[k]:
            grad_x[d, c] = send(send_x, d, recv_x, d, c, at_x)

    def start_y(k):
        if k >= AHEAD:
            sent(grad_y[order_y[k - AHEAD]])
        dz, c = order_y[k]
        grad_y[dz, c] = send(send_y, dz, recv_y, dz, c, at_y)

    def core_part(dz):
        send_c[pl.ds(2 * dz * rows, tile), :] = text_part(dz * 4 + 2).astype(BF16)
        for dy in (1, 0):
            for c in every:
                grad_c[dz, dy, c] = send(send_c, dz * 2 + dy, recv_c, dz * 2 + dy, c, at_core)

    def own_part(dz):
        d_txt[pl.ds(2 * dz * rows, tile), :] = text_part(dz * 4)

    def y_sum(dz, c):
        grad_c[dz, 1, c].wait_recv()
        mine = pl.ds((2 * dz + 1) * rows + c * part, part)
        send_y[pl.ds(dz * rows + c * part, part), :] = (
            d_txt[mine, :] + recv_c[mine, :].astype(F32)
        ).astype(BF16)

    def forward_z(c):
        for d in range(1, far):
            grad_x[d, c].wait_recv()
            mine = pl.ds(d * rows + c * part, part)
            send_z[mine, :] = (d_img[mine, :] + recv_x[mine, :].astype(F32)).astype(BF16)
            grad_z[d, c] = send(send_z, d, recv_z, far - d, c, at_far[d])

    def forward_near(c):
        grad_c[1, 0, c].wait_recv()
        grad_y[1, c].wait_recv()
        mine = pl.ds(2 * rows + c * part, part)
        here = pl.ds(c * part, part)
        send_w[here, :] = (
            d_txt[mine, :]
            + recv_c[mine, :].astype(F32)
            + recv_y[pl.ds(rows + c * part, part), :].astype(F32)
        ).astype(BF16)
        grad_w[c] = send(send_w, 0, recv_w, 0, c, at_near)

    for_tiles(1, far, far_tiles)
    for c in every:
        start_x(c)
    lines, columns = pl.ds(0, tile), pl.ds(2 * tile, 2 * tile)
    coup[lines, columns] = sigmoid_tile(lines, columns).astype(BF16)
    core_part(1)
    own_part(1)
    for c in every:
        y_sum(1, c)
        start_y(c)
    image_part(0)
    for c in range(CHUNKS // 2):
        forward_z(c)
        start_x(CHUNKS + c)
    core_part(0)
    for c in range(CHUNKS // 2, CHUNKS):
        forward_z(c)
        start_x(CHUNKS + c)
    own_part(0)
    for c in every:
        y_sum(0, c)
        start_y(CHUNKS + c)
        forward_near(c)

    samples = rows * pairs
    derivative = adjoint_ref[0] * multiplier / samples
    for c in every:
        here = pl.ds(c * part, part)
        grad_x[0, c].wait_recv()
        total = d_img[here, :] + recv_x[here, :].astype(F32)
        for d in range(1, far):
            grad_z[d, c].wait_recv()
            total += recv_z[pl.ds((far - d) * rows + c * part, part), :].astype(F32)
        unit, scale = unit_rows(picture_ref[here, :])
        image_grad_ref[here, :] = unit_grad(unit, scale, derivative * total)
        grad_c[0, 0, c].wait_recv()
        grad_y[0, c].wait_recv()
        grad_w[c].wait_recv()
        total = (
            d_txt[here, :]
            + recv_c[here, :].astype(F32)
            + recv_y[here, :].astype(F32)
            + recv_w[here, :].astype(F32)
        )
        unit, scale = unit_rows(caption_ref[here, :])
        text_grad_ref[here, :] = unit_grad(unit, scale, derivative * total)
    for copy in started.values():
        if copy is not None:
            copy.wait_send()


def on_device(far, pairs, picture, caption, multiplier, offset, adjoint):
    rows, width = picture.shape
    copies = CHUNKS * (4 * far + 12)
    vmem = pl.BlockSpec(memory_space=pltpu.VMEM)
    hbm = pl.BlockSpec(memory_space=pltpu.HBM)
    smem = pl.BlockSpec(memory_space=pltpu.SMEM)

    def slots(count, kind=BF16):
        return pltpu.VMEM((count * rows, width), kind)

    out = jax.ShapeDtypeStruct((rows, width), F32)
    grads = pl.pallas_call(
        functools.partial(kernel, far, pairs),
        out_shape=(out, out),
        in_specs=[hbm, hbm, smem, smem, smem],
        out_specs=(vmem, vmem),
        scratch_shapes=[
            slots(1),
            slots(1),
            slots(2 * far),
            slots(8),
            pltpu.VMEM((2 * far * rows, 8 * rows), BF16),
            slots(far, F32),
            slots(4, F32),
            slots(far),
            slots(far),
            slots(far),
            slots(far),
            slots(4),
            slots(4),
            slots(2),
            slots(2),
            slots(1),
            slots(1),
            pltpu.SemaphoreType.DMA((2,)),
            pltpu.SemaphoreType.DMA((copies,)),
            pltpu.SemaphoreType.DMA((copies,)),
        ],
        compiler_params=pltpu.CompilerParams(
            collective_id=0, has_side_effects=True, vmem_limit_bytes=52 * 1024 * 1024
        ),
    )(
        pltpu.with_memory_space_constraint(picture, pltpu.HBM),
        pltpu.with_memory_space_constraint(caption, pltpu.HBM),
        multiplier,
        offset,
        adjoint,
    )
    return copied_out(*grads)


def copy_out_kernel(image_ref, text_ref, image_out, text_out, sem):
    copies = [
        pltpu.make_async_copy(image_ref, image_out, sem.at[0]),
        pltpu.make_async_copy(text_ref, text_out, sem.at[1]),
    ]
    for copy in copies:
        copy.start()
    for copy in copies:
        copy.wait()


def copied_out(image_grad, text_grad):
    hbm = pl.BlockSpec(memory_space=pltpu.HBM)
    anywhere = pl.BlockSpec(memory_space=pl.ANY)
    return pl.pallas_call(
        copy_out_kernel,
        out_shape=(
            jax.ShapeDtypeStruct(image_grad.shape, F32),
            jax.ShapeDtypeStruct(text_grad.shape, F32),
        ),
        in_specs=[anywhere, anywhere],
        out_specs=(hbm, hbm),
        scratch_shapes=[pltpu.SemaphoreType.DMA((2,))],
        compiler_params=pltpu.CompilerParams(vmem_limit_bytes=4 * 1024 * 1024),
    )(image_grad, text_grad)


def solution(mesh):
    placed = (P(("blk", "grp"), None), P(("blk", "grp"), None), P(), P(), P())
    pairs = mesh.shape["blk"] * mesh.shape["grp"]
    far = mesh.shape["grp"] // 4
    return jax.shard_map(
        functools.partial(on_device, far, pairs),
        mesh=mesh,
        in_specs=placed,
        out_specs=(P(("blk", "grp"), None), P(("blk", "grp"), None)),
        check_vma=False,
    )
```
